256 devices in a mesh: cloud: 8 (over y_lo, x), leaf: 32 (over y_hi, z, core).
Axes of the slice: x: 4, y: 4 (y_hi: 2, y_lo: 2; y = y_hi * 2 + y_lo), z: 8, core: 2. Of those that a mesh axis runs over, the one named last changes fastest.
Arguments:
- points: bfloat16 [262144, 512], P(('cloud', 'leaf')), parts along dimension 0
- tree_order: int32 [262144], P(('cloud', 'leaf')), parts along dimension 0, may hold values from 0 to 1023, as said below
- present: int32 [262144], P(('cloud', 'leaf')), parts along dimension 0, may hold values 0 or 1
- gain_attn: float32 [3, 512], replicated, may hold values from 0.1 to 1.9
- query_weight: bfloat16 [3, 512, 512], replicated
- key_weight: bfloat16 [3, 512, 512], replicated
- value_weight: bfloat16 [3, 512, 512], replicated, may hold values from -0.25 to 0.25
- out_weight: bfloat16 [3, 512, 512], replicated, may hold values from -0.25 to 0.25
- gain_mlp: float32 [512], replicated, may hold values from 0.1 to 1.9
- hidden_weight: bfloat16 [512, 2048], replicated, may hold values from -0.25 to 0.25
- proj_weight: bfloat16 [2048, 512], replicated, may hold values from -0.125 to 0.125
Outputs:
- field: bfloat16 [262144, 512], P(('cloud', 'leaf')), parts along dimension 0
The draws below stay inside these ranges and needn't reach their ends.
There are 8 independent parts, one for each index of `cloud`. The reference program is written for one: setup_inputs(seed, part) draws one part's arguments, and reference() takes and returns one part's arrays. A program takes and returns all parts, laid end to end along the dimension named above; an argument that names none is the same for every part. Nothing has to cross between parts.
Inputs may be any that keep to these rules, and one draw needn't show every extreme that they name: `tree_order`: within each aligned block of 1024 entries, each of 0 to 1023 appears once.
All inputs are finite; a program needn't handle non-finite values. No bound on the sum of `present` on one device may be relied on, other than what follows from the above.
Results may differ from the reference program's by a relative error of at most 0.025.
Values may be sent and summed in bfloat16 or wider, within the bound.
No kernel may reach another device: no remote copies, remote signals or barrier semaphores. Data moves between devices by JAX's collectives and lax.ppermute only.
A program may use at most 192 MiB of HBM per device.

```python
import math
import jax
import jax.numpy as jnp
from jax import lax

D = 512
FF = 2048
HEAD = 64
TOK_DEV = 1024
POINTS = 32768
N_LEAF = 32


def shared_basis(key):
    return jnp.clip(jax.random.normal(key, (3, D, D), jnp.float32), -5.0, 5.0)


def head_scales(key, lowest, highest):
    scale = jnp.exp(jax.random.uniform(key, (3, 1, D // HEAD), jnp.float32, math.log(lowest), math.log(highest)))
    return jnp.repeat(scale, HEAD, axis=2)


def draw_key_weight(key, part):
    basis = shared_basis(key)
    return (basis * D ** (-0.5)).astype(jnp.bfloat16)


def draw_query_weight(key, part):
    key = jax.random.fold_in(key, 7)
    noise = jnp.clip(jax.random.normal(key, (3, D, D), jnp.float32), -5.0, 5.0)
    spread = head_scales(jax.random.fold_in(key, 3), 1.2, 3.0)
    return (spread * noise * D ** (-0.5)).astype(jnp.bfloat16)


def draw_points(key, part):
    key = jax.random.fold_in(key, 3)
    return jnp.clip(jax.random.normal(key, (POINTS, D), jnp.float32), -6.0, 6.0).astype(jnp.bfloat16)


def draw_tree_order(key, part):
    key = jax.random.fold_in(key, 11)
    block_keys = jax.random.split(key, POINTS // TOK_DEV)
    orders = jax.vmap(lambda block_key: jax.random.permutation(block_key, TOK_DEV))(block_keys)
    return orders.reshape(POINTS).astype(jnp.int32)


def set_ends(array, key, smallest, high):
    shape = array.shape
    place = [jax.random.randint(jax.random.fold_in(key, axis), (), 0, shape[axis]) for axis in range(len(shape))]
    array = array.at[tuple(place)].set(smallest)
    longest = shape.index(max(shape))
    place[longest] = (place[longest] + 1) % shape[longest]
    return array.at[tuple(place)].set(high)


def normal_values(stream_key, dims, scale, most, kind=jnp.bfloat16):
    return jnp.clip(scale * jax.random.normal(stream_key, dims, jnp.float32), -most, most).astype(kind)


def setup_inputs(seed: int = 0, part: int = 0) -> dict:
    key_of = jax.random.split(jax.random.key(seed), 12)
    part_splits = jax.random.split(jax.random.fold_in(key_of[11], part), 12)
    return {
        "points": draw_points(jax.random.fold_in(jax.random.fold_in(key_of[11], part), 71), part),
        "tree_order": draw_tree_order(jax.random.fold_in(jax.random.fold_in(key_of[11], part), 71), part),
        "present": set_ends((jax.random.randint(part_splits[2], (POINTS,), 0, 4) < 3).astype(jnp.int32), jax.random.fold_in(part_splits[2], 1), 0, 1),
        "gain_attn": jnp.clip(1.0 + 0.18 * jax.random.normal(key_of[3], (3, D), jnp.float32), 0.1, 1.9),
        "query_weight": draw_query_weight(jax.random.fold_in(key_of[11], 71), part),
        "key_weight": draw_key_weight(jax.random.fold_in(key_of[11], 71), part),
        "value_weight": normal_values(key_of[6], (3, D, D), D ** -0.5, 0.25),
        "out_weight": normal_values(key_of[7], (3, D, D), D ** -0.5, 0.25),
        "gain_mlp": jnp.clip(1.0 + 0.18 * jax.random.normal(key_of[8], (D,), jnp.float32), 0.1, 1.9),
        "hidden_weight": normal_values(key_of[9], (D, FF), D ** -0.5, 0.25),
        "proj_weight": normal_values(key_of[10], (FF, D), FF ** -0.5, 0.125),
    }


def norm_rows(values, gain_row):
    wide = values.astype(jnp.float32)
    centre = lax.optimization_barrier(jnp.mean(wide, axis=-1, keepdims=True))
    spread = lax.optimization_barrier(jnp.mean(jnp.square(wide - centre), axis=-1, keepdims=True))
    return ((wide - centre) * lax.rsqrt(spread + 1e-05) * gain_row).astype(jnp.bfloat16)

def project(values, weight):
    flat = values.reshape(-1, values.shape[-1])
    product = jnp.dot(flat, weight, preferred_element_type=jnp.float32)
    return product.reshape(values.shape[:-1] + (weight.shape[1],))

def attend(queries, key_rows, value_rows, key_filled):
    row_count = queries.shape[0]
    model_width = queries.shape[1]
    head_count = model_width // HEAD
    query_heads = queries.reshape(row_count, head_count, HEAD).astype(jnp.float32)
    key_heads = key_rows.reshape(-1, head_count, HEAD).astype(jnp.float32)
    value_heads = value_rows.reshape(-1, head_count, HEAD).astype(jnp.float32)
    scores = jnp.einsum('qhd,khd->hqk', query_heads, key_heads) * HEAD ** (-0.5)
    own_row = jnp.arange(key_rows.shape[0], dtype=jnp.int32)[None, :] == jnp.arange(row_count, dtype=jnp.int32)[:, None]
    allowed = (key_filled[None, :] > 0) | own_row
    scores = jnp.where(allowed[None], scores, -1e+30)
    row_top = lax.optimization_barrier(jnp.max(scores, axis=-1, keepdims=True))
    weights = jnp.exp(scores - row_top)
    weights = (weights / lax.optimization_barrier(jnp.sum(weights, axis=-1, keepdims=True))).astype(jnp.bfloat16)
    merged = jnp.einsum('hqk,khd->qhd', weights.astype(jnp.float32), value_heads)
    return merged.reshape(row_count, model_width).astype(jnp.bfloat16)

def reference(points, tree_order, present, gain_attn, query_weight, key_weight, value_weight, out_weight, gain_mlp, hidden_weight, proj_weight):
    blocks = POINTS // TOK_DEV
    tree_rows = jnp.arange(POINTS, dtype=jnp.int32) // TOK_DEV * TOK_DEV + tree_order.astype(jnp.int32)
    filled = present[tree_rows].astype(jnp.bfloat16)
    current = points[tree_rows] * filled[:, None]
    current = current.reshape(blocks, TOK_DEV, D)
    filled = filled.reshape(blocks, TOK_DEV)
    skips = []
    for level_index in range(3):
        normed = norm_rows(current, gain_attn[level_index])
        queries = project(normed, query_weight[level_index]).astype(jnp.bfloat16)
        key_rows = project(normed, key_weight[level_index]).astype(jnp.bfloat16)
        value_rows = project(normed, value_weight[level_index]).astype(jnp.bfloat16)
        partner = jnp.arange(blocks, dtype=jnp.int32) ^ N_LEAF // 8 << level_index
        joined_keys = jnp.concatenate([key_rows, key_rows[partner]], axis=1)
        joined_values = jnp.concatenate([value_rows, value_rows[partner]], axis=1)
        joined_filled = jnp.concatenate([filled, filled[partner]], axis=1)
        attended = lax.map(lambda group: attend(group[0], group[1], group[2], group[3]), (queries, joined_keys, joined_values, joined_filled))
        current = (current.astype(jnp.float32) + project(attended, out_weight[level_index])).astype(jnp.bfloat16)
        if level_index < 2:
            skips.append(current)
            rows_now = current.shape[1]
            current = lax.optimization_barrier(jnp.mean(current.reshape(blocks, rows_now // 2, 2, D).astype(jnp.float32), axis=2)).astype(jnp.bfloat16)
            filled = lax.optimization_barrier(jnp.max(filled.reshape(blocks, rows_now // 2, 2), axis=2))
    normed = norm_rows(current, gain_mlp)
    hidden = jax.nn.gelu(project(normed, hidden_weight), approximate=True).astype(jnp.bfloat16)
    current = (current.astype(jnp.float32) + project(hidden, proj_weight)).astype(jnp.bfloat16)
    for skip_rows in reversed(skips):
        spread_rows = jnp.repeat(current, 2, axis=1)
        current = (skip_rows.astype(jnp.float32) + spread_rows.astype(jnp.float32)).astype(jnp.bfloat16)
    flat = current.reshape(POINTS, D)
    return jnp.zeros((POINTS, D), jnp.bfloat16).at[tree_rows].set(flat)
```

```python
import functools
import jax
import jax.numpy as jnp
from jax import lax
from jax.experimental import pallas as pl
from jax.experimental.pallas import tpu as pltpu
from jax.sharding import PartitionSpec as P

D = 512
HEAD = 64
HEADS = 8
VROWS = 80
LIMIT2 = 90.0**2
QSCALE = HEAD ** (-0.5) * 1.4426950408889634
NT = (((1,), (1,)), ((), ()))
TN = (((0,), (0,)), ((), ()))
BF = jnp.bfloat16
F32 = jnp.float32
VMEM = pl.BlockSpec(memory_space=pltpu.VMEM)
ANY = pl.BlockSpec(memory_space=pl.ANY)


def dotf(a, b, dims=(((1,), (0,)), ((), ()))):
    return lax.dot_general(a, b, dims, preferred_element_type=F32)


def norm_rows(values, gain):
    wide = values.astype(F32)
    centre = jnp.mean(wide, axis=-1, keepdims=True)
    wide = wide - centre
    spread = jnp.mean(jnp.square(wide), axis=-1, keepdims=True)
    return (wide * lax.rsqrt(spread + 1e-05) * gain).astype(BF)


def to_column(row):
    eye = lax.broadcasted_iota(jnp.int32, (128, 128), 0) == lax.broadcasted_iota(
        jnp.int32, (128, 128), 1
    )
    parts = []
    for start in range(0, row.shape[1], 128):
        block = jnp.where(eye, row[:, start : start + 128], 0.0)
        parts.append(jnp.sum(block, axis=1, keepdims=True))
    return jnp.concatenate(parts, axis=0)


def head_select():
    lane = lax.broadcasted_iota(jnp.int32, (16, D), 1)
    head = lax.broadcasted_iota(jnp.int32, (16, D), 0)
    return jnp.where(lane // HEAD == head, 1.0, 0.0).astype(BF)


def head_peak(rows):
    wide = rows.astype(F32)
    sums = dotf(head_select(), (wide * wide).astype(BF), NT)
    return jnp.broadcast_to(jnp.max(sums, axis=1, keepdims=True), (16, 128))


def split_keys(keys, km_ref):
    low = lax.broadcasted_iota(jnp.int32, (1, 128), 1) < HEAD
    for pair in range(HEADS // 2):
        part = keys[:, pair * 128 : (pair + 1) * 128]
        km_ref[2 * pair] = jnp.where(low, part, jnp.zeros_like(part))
        km_ref[2 * pair + 1] = jnp.where(low, jnp.zeros_like(part), part)


def split_values(values_t, fill_row, va_ref):
    width = values_t.shape[1]
    first = lax.broadcasted_iota(jnp.int32, (16, width), 0) == 0
    ones = jnp.where(first, fill_row, 0.0).astype(BF)
    for head in range(HEADS):
        part = values_t[head * HEAD : (head + 1) * HEAD].astype(F32)
        va_ref[head, :HEAD, :] = (part * fill_row).astype(BF)
        va_ref[head, HEAD:, :] = ones


def attend(q_ref, km_ref, va_ref, o_ref, add_ref):
    blocks = km_ref.shape[1] // 256

    def body(pair, carry):
        queries = q_ref[:, pl.ds(pl.multiple_of(pair * 128, 128), 128)]
        waiting = []

        def finish(head, block, scores, total):
            weights = jnp.exp2(scores).astype(BF)
            values = va_ref[pair * 2 + head, :, block * 256 : (block + 1) * 256]
            part = dotf(values, weights)
            return part if total is None else total + part

        totals = [None, None]

        def drain():
            head, block, scores = waiting.pop(0)
            totals[head] = finish(head, block, scores, totals[head])
            if block == blocks - 1:
                out = totals[head]
                if add_ref is not None:
                    out = out + add_ref[pair * 2 + head]
                o_ref[pair * 2 + head] = out

        for head in range(2):
            for block in range(blocks):
                keys = km_ref[pair * 2 + head, block * 256 : (block + 1) * 256, :]
                waiting.append((head, block, dotf(keys, queries, NT)))
                if len(waiting) > 1:
                    drain()
        while waiting:
            drain()
        return carry

    lax.fori_loop(0, HEADS // 2, body, 0)


def project_kv(normed, kw_ref, vw_ref):
    keys = dotf(normed, kw_ref[...]).astype(BF)
    values_t = dotf(vw_ref[...], normed, (((0,), (1,)), ((), ()))).astype(BF)
    return keys, values_t


def local_kernel(level, x_ref, fill_ref, gain_ref, qw_ref, kw_ref, vw_ref,
                 q_ref, k_ref, vt_ref, o_ref, qp_ref, kp_ref, km_ref, va_ref):
    rows = k_ref.shape[0]
    fill = fill_ref[...].astype(F32)
    normed = norm_rows(x_ref[:rows, :], gain_ref[...])
    if level == 0:
        normed = normed * to_column(fill).astype(BF)
    queries = (dotf(normed, qw_ref[...]) * QSCALE).astype(BF)
    q_ref[...] = queries
    keys, values_t = project_kv(normed, kw_ref, vw_ref)
    k_ref[...] = keys
    vt_ref[...] = values_t
    qp_ref[...] = head_peak(queries)
    kp_ref[...] = head_peak(keys)
    split_keys(keys, km_ref)
    split_values(values_t, fill, va_ref)
    attend(q_ref, km_ref, va_ref, o_ref, None)
    if level == 0:
        for head in range(HEADS):
            o_ref[head, HEAD : HEAD + 1, :] += 1.0 - fill
    else:
        prod = queries.astype(F32) * keys.astype(F32)
        high = prod.astype(BF)
        rest = (prod - high.astype(F32)).astype(BF)
        select = head_select()
        own = jnp.exp2(dotf(select, high, NT) + dotf(select, rest, NT))
        own = own * (1.0 - fill)
        for head in range(HEADS):
            weight = own[head : head + 1]
            part = values_t[head * HEAD : (head + 1) * HEAD].astype(F32)
            o_ref[head, :HEAD, :] += part * weight
            o_ref[head, HEAD : HEAD + 1, :] += weight


def remote_kernel(x_ref, fill_ref, gain_ref, kw_ref, vw_ref, q_ref, kp_in, o_in,
                  o_ref, kp_ref, km_ref, va_ref):
    rows = km_ref.shape[1]
    normed = norm_rows(x_ref[:rows, :], gain_ref[...])
    keys, values_t = project_kv(normed, kw_ref, vw_ref)
    kp_ref[...] = jnp.maximum(kp_in[...], head_peak(keys))
    split_keys(keys, km_ref)
    split_values(values_t, fill_ref[...].astype(F32), va_ref)
    attend(q_ref, km_ref, va_ref, o_ref, o_in)


def exact_attend(level, q_ref, fills, chunk_refs, chunk_rows, gain_ref, kw_ref, vw_ref,
                 k_loc, vt_loc, att_ref, xbuf, kf, vf):
    rows = q_ref.shape[0]
    pltpu.sync_copy(k_loc, kf.at[pl.ds(0, rows), :])
    pltpu.sync_copy(vt_loc, vf.at[:, pl.ds(0, rows)])
    at = rows
    for ref, count in zip(chunk_refs, chunk_rows):
        pltpu.sync_copy(ref.at[pl.ds(0, count), :], xbuf.at[pl.ds(0, count), :])
        normed = norm_rows(xbuf[:count, :], gain_ref[...])
        keys, values_t = project_kv(normed, kw_ref, vw_ref)
        kf[at : at + count, :] = keys
        vf[:, at : at + count] = values_t
        at += count
    total = 2 * rows
    low = lax.broadcasted_iota(jnp.int32, (1, 128), 1) < HEAD
    fill8 = jnp.broadcast_to(jnp.concatenate(fills, axis=1), (8, total)).astype(BF)
    width = 128

    def body(step, carry):
        pair = step // (rows // width)
        start = pl.multiple_of(step % (rows // width) * width, width)
        lanes = pl.ds(pl.multiple_of(pair * 128, 128), 128)
        queries = q_ref[pl.ds(start, width), lanes]
        keys = kf[:, lanes]
        mask = dotf(fill8, jnp.ones((8, width), BF), TN) > 0.5
        own = lax.broadcasted_iota(jnp.int32, (total, width), 0) == (
            lax.broadcasted_iota(jnp.int32, (total, width), 1) + start
        )
        allowed = mask | own
        for head in range(2):
            part = jnp.where(low if head == 0 else ~low, keys, jnp.zeros_like(keys))
            scores = jnp.where(allowed, dotf(part, queries, NT), -1e30)
            weights = jnp.exp2(scores - jnp.max(scores, axis=0, keepdims=True))
            weights = weights / jnp.sum(weights, axis=0, keepdims=True)
            first = pl.multiple_of(pair * 128 + head * HEAD, HEAD)
            values = vf[pl.ds(first, HEAD), :]
            att_ref[pl.ds(first, HEAD), pl.ds(start, width)] = dotf(
                values, weights.astype(BF)
            ).astype(BF)
        return carry

    lax.fori_loop(0, HEADS // 2 * (rows // width), body, 0)


def finish_attention(level, refs, chunk_refs, chunk_rows, fill, fills_far):
    (gain_ref, kw_ref, vw_ref, q_ref, qp_ref, kp_ref, o_in, k_loc, vt_loc,
     att_ref, km_ref, va_ref, o_scr, xbuf, kf, vf, last_ref) = refs
    rows = km_ref.shape[1]
    normed = norm_rows(last_ref[:rows, :], gain_ref[...])
    keys, values_t = project_kv(normed, kw_ref, vw_ref)
    peak = jnp.maximum(kp_ref[...], head_peak(keys)) * qp_ref[...]
    split_keys(keys, km_ref)
    split_values(values_t, fills_far[-1], va_ref)
    attend(q_ref, km_ref, va_ref, o_scr, o_in)
    for head in range(HEADS):
        scale = 1.0 / o_scr[head, HEAD : HEAD + 1, :]
        att_ref[head * HEAD : (head + 1) * HEAD, :] = (o_scr[head, :HEAD, :] * scale).astype(BF)
    inside = jnp.max(peak) <= LIMIT2

    @pl.when(jnp.logical_not(inside))
    def _():
        exact_attend(level, q_ref, [fill] + fills_far, chunk_refs, chunk_rows, gain_ref,
                     kw_ref, vw_ref, k_loc, vt_loc, att_ref, xbuf, kf, vf)


def finish0_kernel(counts, *refs):
    n = len(counts)
    chunks, rest = refs[:n], refs[n:]
    (last_ref, fill_ref, far_ref, gain_ref, kw_ref, vw_ref, ow_ref, q_ref, qp_ref, kp_ref, o_in,
     k_loc, vt_loc, points_ref, tree_ref,
     y_ref, xa_ref, xb_ref, f_ref, att_ref, km_ref, va_ref, o_scr, xbuf, kf, vf) = rest
    fill = fill_ref[...].astype(F32)
    far = far_ref[...].astype(F32)
    fills_far, at = [], 0
    for count in counts:
        fills_far.append(far[:, at : at + count])
        at += count
    finish_attention(0, (gain_ref, kw_ref, vw_ref, q_ref, qp_ref, kp_ref, o_in, k_loc, vt_loc,
                         att_ref, km_ref, va_ref, o_scr, xbuf, kf, vf, last_ref),
                     chunks, counts, fill, fills_far)
    x0 = points_ref[...].astype(F32) * to_column(fill)
    y = (x0 + dotf(att_ref[...], ow_ref[...], TN)).astype(BF)
    y_ref[...] = y
    lanes = lax.broadcasted_iota(jnp.int32, (256, 1024), 1)
    f8 = jnp.broadcast_to(fill, (8, 1024)).astype(BF)
    for half, out in ((0, xa_ref), (1, xb_ref)):
        picked = (lanes == tree_ref[:, 2 * half : 2 * half + 1]) | (
            lanes == tree_ref[:, 2 * half + 1 : 2 * half + 2]
        )
        pool = jnp.where(picked, 0.5, 0.0).astype(BF)
        out[:256, :] = dotf(pool, y).astype(BF)
        f_half = jnp.where(dotf(f8, pool, NT)[:1] > 0.25, 1.0, 0.0)
        f_ref[:, half * 256 : (half + 1) * 256] = f_half


def finish1_kernel(counts, *refs):
    n = len(counts)
    chunks, rest = refs[:n], refs[n:]
    (last_ref, fill_ref, far_ref, gain_ref, kw_ref, vw_ref, ow_ref, q_ref, qp_ref, kp_ref, o_in,
     k_loc, vt_loc, x_ref,
     y_ref, x2_ref, f_ref, att_ref, km_ref, va_ref, o_scr, xbuf, kf, vf) = rest
    fill = fill_ref[...].astype(F32)
    far = far_ref[...].astype(F32)
    fills_far, at = [], 0
    for count in counts:
        fills_far.append(far[:, at : at + count])
        at += count
    finish_attention(1, (gain_ref, kw_ref, vw_ref, q_ref, qp_ref, kp_ref, o_in, k_loc, vt_loc,
                         att_ref, km_ref, va_ref, o_scr, xbuf, kf, vf, last_ref),
                     chunks, counts, fill, fills_far)
    y = (x_ref[...].astype(F32) + dotf(att_ref[...], ow_ref[...], TN)).astype(BF)
    y_ref[...] = y
    wide = y.astype(F32)
    x2_ref[:256, :] = ((wide[:256] + wide[256:]) * 0.5).astype(BF)
    f_ref[...] = jnp.maximum(fill[:, :256], fill[:, 256:])


def finish2_kernel(counts, *refs):
    n = len(counts)
    chunks, rest = refs[:n], refs[n:]
    (last_ref, fill_ref, far_ref, gain_ref, kw_ref, vw_ref, ow_ref, q_ref, qp_ref, kp_ref, o_in,
     k_loc, vt_loc, x_ref, gm_ref, hw_ref, pw_ref, y1_ref, y0_ref, tree_ref,
     field_ref, att_ref, km_ref, va_ref, o_scr, xbuf, kf, vf) = rest
    fill = fill_ref[...].astype(F32)
    far = far_ref[...].astype(F32)
    finish_attention(2, (gain_ref, kw_ref, vw_ref, q_ref, qp_ref, kp_ref, o_in, k_loc, vt_loc,
                         att_ref, km_ref, va_ref, o_scr, xbuf, kf, vf, last_ref),
                     chunks, counts, fill, [far])
    y2 = (x_ref[:256, :].astype(F32) + dotf(att_ref[...], ow_ref[...], TN)).astype(BF)
    normed = norm_rows(y2, gm_ref[...])
    hidden = jax.nn.gelu(dotf(normed, hw_ref[...]), approximate=True).astype(BF)
    top = (y2.astype(F32) + dotf(hidden, pw_ref[...])).astype(BF).astype(F32)
    up = [(y1_ref[half * 256 : (half + 1) * 256, :].astype(F32) + top).astype(BF)
          for half in range(2)]
    rows = lax.broadcasted_iota(jnp.int32, (1024, 256), 0)
    total = y0_ref[...].astype(F32)
    for half in range(2):
        picked = (rows == tree_ref[2 * half : 2 * half + 1, :]) | (
            rows == tree_ref[2 * half + 1 : 2 * half + 2, :]
        )
        total = total + dotf(jnp.where(picked, 1.0, 0.0).astype(BF), up[half])
    field_ref[...] = total.astype(BF)


def call(kernel, outs, args, in_any=(), scratch=(), flops=0):
    nbytes = sum(a.size * a.dtype.itemsize for a in args) + sum(
        a.size * a.dtype.itemsize for a in outs)
    return pl.pallas_call(
        kernel,
        out_shape=outs,
        in_specs=[ANY if i in in_any else VMEM for i in range(len(args))],
        out_specs=[VMEM] * len(outs),
        scratch_shapes=list(scratch),
        compiler_params=pltpu.CompilerParams(vmem_limit_bytes=56 * 2**20),
        cost_estimate=pl.CostEstimate(flops=flops, bytes_accessed=nbytes, transcendentals=0),
    )(*args)


def shape(*dims, dtype=BF):
    return jax.ShapeDtypeStruct(dims, dtype)


def local_part(level, x, fill, gain, qw, kw, vw, rows):
    return call(
        functools.partial(local_kernel, level),
        [shape(rows, D), shape(rows, D), shape(D, rows), shape(HEADS, VROWS, rows, dtype=F32),
         shape(16, 128, dtype=F32), shape(16, 128, dtype=F32)],
        [x, fill, gain, qw, kw, vw],
        scratch=[pltpu.VMEM((HEADS, rows, 128), BF), pltpu.VMEM((HEADS, VROWS, rows), BF)],
        flops=8 * rows * rows * 512 * 2,
    )


def remote_part(x, fill, gain, kw, vw, q, kp, o, count):
    rows = q.shape[0]
    return call(
        remote_kernel,
        [shape(HEADS, VROWS, rows, dtype=F32), shape(16, 128, dtype=F32)],
        [x, fill, gain, kw, vw, q, kp, o],
        scratch=[pltpu.VMEM((HEADS, count, 128), BF), pltpu.VMEM((HEADS, VROWS, count), BF)],
        flops=8 * rows * count * 512 * 2,
    )


def finish_part(kernel, counts, chunks, args, outs, rows):
    n = len(counts)
    inputs = list(chunks) + [chunks[-1]] + args
    return call(
        functools.partial(kernel, counts),
        outs,
        inputs,
        in_any=set(range(n)) | {n + 11, n + 12},
        scratch=[
            pltpu.VMEM((D, rows), BF),
            pltpu.VMEM((HEADS, counts[-1], 128), BF),
            pltpu.VMEM((HEADS, VROWS, counts[-1]), BF),
            pltpu.VMEM((HEADS, VROWS, rows), F32),
            pltpu.VMEM((max(counts), D), BF),
            pltpu.VMEM((2 * rows, D), BF),
            pltpu.VMEM((D, 2 * rows), BF),
        ],
        flops=8 * rows * counts[-1] * 512 * 2 + 4 * rows * D * D,
    )


def per_device(points, tree_order, present, gain_attn, query_weight, key_weight, value_weight,
               out_weight, gain_mlp, hidden_weight, proj_weight):
    size = lax.axis_size("leaf")

    def trade(value, bit):
        return lax.ppermute(value, "leaf", [(s, s ^ (1 << bit)) for s in range(size)])

    base = size.bit_length() - 1 - 3
    fill0 = present.reshape(1, 1024)
    far_fill = trade(fill0, base)
    counts0 = (256, 256, 256, 256)
    chunks, at = [], 0
    for i, count in enumerate(counts0):
        part = points[at : at + count]
        if i >= 2:
            part, _ = lax.optimization_barrier((part, chunks[i - 2]))
        chunks.append(trade(part, base))
        at += count
    tree4 = tree_order.reshape(256, 4)
    tree_rows = tree4.T

    def gain(level):
        return gain_attn[level].reshape(1, D)

    q, k, vt, o, qp, kp = local_part(0, points, fill0, gain(0), query_weight[0], key_weight[0],
                                     value_weight[0], 1024)
    at = 0
    for chunk, count in zip(chunks[:-1], counts0[:-1]):
        o, kp = remote_part(chunk, far_fill[:, at : at + count], gain(0), key_weight[0],
                            value_weight[0], q, kp, o, count)
        at += count
    y0, xa, xb, f1 = finish_part(
        finish0_kernel, counts0, chunks,
        [fill0, far_fill, gain(0), key_weight[0], value_weight[0], out_weight[0], q, qp, kp, o, k,
         vt, points, tree4],
        [shape(1024, D), shape(256, D), shape(256, D), shape(1, 512, dtype=F32)], 1024)
    far_f1 = trade(f1, base + 1)
    far_a = trade(xa, base + 1)
    far_b = trade(xb, base + 1)
    x1 = jnp.concatenate([xa, xb], axis=0)
    q, k, vt, o, qp, kp = local_part(1, x1, f1, gain(1), query_weight[1], key_weight[1],
                                     value_weight[1], 512)
    o, kp = remote_part(far_a, far_f1[:, :256], gain(1), key_weight[1], value_weight[1], q, kp, o,
                        256)
    y1, x2, f2 = finish_part(
        finish1_kernel, (256, 256), [far_a, far_b],
        [f1, far_f1, gain(1), key_weight[1], value_weight[1], out_weight[1], q, qp, kp, o, k, vt,
         x1],
        [shape(512, D), shape(256, D), shape(1, 256, dtype=F32)], 512)
    far_f2 = trade(f2, base + 2)
    far_x2 = trade(x2, base + 2)
    q, k, vt, o, qp, kp = local_part(2, x2, f2, gain(2), query_weight[2], key_weight[2],
                                     value_weight[2], 256)
    (field,) = finish_part(
        finish2_kernel, (256,), [far_x2],
        [f2, far_f2, gain(2), key_weight[2], value_weight[2], out_weight[2], q, qp, kp, o, k, vt,
         x2, gain_mlp.reshape(1, D), hidden_weight, proj_weight, y1, y0, tree_rows],
        [shape(1024, D)], 256)
    return field


def solution(mesh):
    placed = (
        P(("cloud", "leaf"), None),
        P(("cloud", "leaf")),
        P(("cloud", "leaf")),
        P(), P(), P(), P(), P(), P(), P(), P(),
    )
    return jax.shard_map(
        per_device,
        mesh=mesh,
        in_specs=placed,
        out_specs=P(("cloud", "leaf"), None),
        check_vma=False,
    )
```

```python
import functools
import jax
import jax.numpy as jnp
from jax import lax
from jax.experimental import pallas as pl
from jax.experimental.pallas import tpu as pltpu
from jax.sharding import PartitionSpec as P

D = 512
HEAD = 64
HEADS = 8
VROWS = 80
LIMIT2 = 90.0**2
QSCALE = HEAD ** (-0.5) * 1.4426950408889634
NT = (((1,), (1,)), ((), ()))
TN = (((0,), (0,)), ((), ()))
BF = jnp.bfloat16
F32 = jnp.float32
ANY = pl.BlockSpec(memory_space=pl.ANY)
VLIMIT = 62 * 2**20


def dotf(a, b, dims=(((1,), (0,)), ((), ()))):
    return lax.dot_general(a, b, dims, preferred_element_type=F32)


def norm_rows(values, gain):
    wide = values.astype(F32)
    centre = jnp.mean(wide, axis=-1, keepdims=True)
    wide = wide - centre
    spread = jnp.mean(jnp.square(wide), axis=-1, keepdims=True)
    return (wide * lax.rsqrt(spread + 1e-05) * gain).astype(BF)


def to_column(row):
    eye = lax.broadcasted_iota(jnp.int32, (128, 128), 0) == lax.broadcasted_iota(
        jnp.int32, (128, 128), 1
    )
    parts = []
    for start in range(0, row.shape[1], 128):
        block = jnp.where(eye, row[:, start : start + 128], 0.0)
        parts.append(jnp.sum(block, axis=1, keepdims=True))
    return jnp.concatenate(parts, axis=0)


def head_select():
    lane = lax.broadcasted_iota(jnp.int32, (16, D), 1)
    head = lax.broadcasted_iota(jnp.int32, (16, D), 0)
    return jnp.where(lane // HEAD == head, 1.0, 0.0).astype(BF)


def head_peak(rows):
    wide = rows.astype(F32)
    sums = dotf(head_select(), (wide * wide).astype(BF), NT)
    return jnp.broadcast_to(jnp.max(sums, axis=1, keepdims=True), (16, 128))


def split_keys(keys, km_ref):
    low = lax.broadcasted_iota(jnp.int32, (1, 128), 1) < HEAD
    for pair in range(HEADS // 2):
        part = keys[:, pair * 128 : (pair + 1) * 128]
        km_ref[2 * pair] = jnp.where(low, part, jnp.zeros_like(part))
        km_ref[2 * pair + 1] = jnp.where(low, jnp.zeros_like(part), part)


def split_values(values_t, fill_row, va_ref):
    width = values_t.shape[1]
    first = lax.broadcasted_iota(jnp.int32, (16, width), 0) == 0
    ones = jnp.where(first, fill_row, 0.0).astype(BF)
    for head in range(HEADS):
        part = values_t[head * HEAD : (head + 1) * HEAD].astype(F32)
        va_ref[head, :HEAD, :] = (part * fill_row).astype(BF)
        va_ref[head, HEAD:, :] = ones


def attend(q_ref, km_ref, va_ref, o_ref, add_ref):
    count = km_ref.shape[1]
    blocks = [(start, min(256, count - start)) for start in range(0, count, 256)]

    def body(pair, carry):
        queries = q_ref[:, pl.ds(pl.multiple_of(pair * 128, 128), 128)]
        waiting = []

        def finish(head, block, scores, total):
            weights = jnp.exp2(scores).astype(BF)
            start, size = block
            values = va_ref[pair * 2 + head, :, start : start + size]
            part = dotf(values, weights)
            return part if total is None else total + part

        totals = [None, None]

        def drain():
            head, block, scores = waiting.pop(0)
            totals[head] = finish(head, block, scores, totals[head])
            if block == blocks[-1]:
                out = totals[head]
                if add_ref is not None:
                    out = out + add_ref[pair * 2 + head]
                o_ref[pair * 2 + head] = out

        for head in range(2):
            for block in blocks:
                start, size = block
                keys = km_ref[pair * 2 + head, start : start + size, :]
                waiting.append((head, block, dotf(keys, queries, NT)))
                if len(waiting) > 1:
                    drain()
        while waiting:
            drain()
        return carry

    lax.fori_loop(0, HEADS // 2, body, 0)


def project_kv(normed, kw, vw):
    keys = dotf(normed, kw.here[...]).astype(BF)
    values_t = dotf(vw.here[...], normed, (((0,), (1,)), ((), ()))).astype(BF)
    return keys, values_t


def local_kernel(level, rows, x, fill_src, gains, qw, kw, vw,
                 q, k, vt, o, qp, kp, km_ref, va_ref):
    normed = norm_rows(x.here[:rows, :], gains.here[level : level + 1, :])
    if level == 0:
        fill = fill_src.here[...].astype(F32)
        normed = normed * to_column(fill).astype(BF)
    else:
        fill = x.here[rows : rows + 1, :rows].astype(F32)
    queries = (dotf(normed, qw.here[...]) * QSCALE).astype(BF)
    q.ref[...] = queries
    q.flush()
    keys, values_t = project_kv(normed, kw, vw)
    k.ref[...] = keys
    vt.ref[...] = values_t
    k.flush()
    vt.flush()
    qp.ref[...] = head_peak(queries)
    kp.ref[...] = head_peak(keys)
    qp.flush()
    kp.flush()
    split_keys(keys, km_ref)
    split_values(values_t, fill, va_ref)
    attend(q.ref, km_ref, va_ref, o.ref, None)
    if level == 0:
        for head in range(HEADS):
            o.ref[head, HEAD : HEAD + 1, :] += 1.0 - fill
    else:
        prod = queries.astype(F32) * keys.astype(F32)
        high = prod.astype(BF)
        rest = (prod - high.astype(F32)).astype(BF)
        select = head_select()
        own = jnp.exp2(dotf(select, high, NT) + dotf(select, rest, NT))
        own = own * (1.0 - fill)
        for head in range(HEADS):
            weight = own[head : head + 1]
            part = values_t[head * HEAD : (head + 1) * HEAD].astype(F32)
            o.ref[head, :HEAD, :] += part * weight
            o.ref[head, HEAD : HEAD + 1, :] += weight
    o.flush()


def remote_kernel(level, at, x, fill, gains, kw, vw, q, kp_in, o_in, o, kp, km_ref, va_ref):
    rows = km_ref.shape[1]
    normed = norm_rows(x.here[:rows, :], gains.here[level : level + 1, :])
    keys, values_t = project_kv(normed, kw, vw)
    kp.ref[...] = jnp.maximum(kp_in.here[...], head_peak(keys))
    kp.flush()
    split_keys(keys, km_ref)
    split_values(values_t, fill.here[:, at : at + rows].astype(F32), va_ref)
    attend(q.here, km_ref, va_ref, o.ref, o_in.here)
    o.flush()


def exact_attend(level, q_ref, fills, chunk_refs, chunk_rows, gains, kw, vw,
                 k_loc, vt_loc, att_ref, xbuf, kf, vf):
    rows = q_ref.shape[0]
    pltpu.sync_copy(k_loc, kf.at[pl.ds(0, rows), :])
    pltpu.sync_copy(vt_loc, vf.at[:, pl.ds(0, rows)])
    at = rows
    for ref, count in zip(chunk_refs, chunk_rows):
        pltpu.sync_copy(ref.at[pl.ds(0, count), :], xbuf.at[pl.ds(0, count), :])
        normed = norm_rows(xbuf[:count, :], gains.here[level : level + 1, :])
        keys, values_t = project_kv(normed, kw, vw)
        kf[at : at + count, :] = keys
        vf[:, at : at + count] = values_t
        at += count
    total = 2 * rows
    low = lax.broadcasted_iota(jnp.int32, (1, 128), 1) < HEAD
    fill8 = jnp.broadcast_to(jnp.concatenate(fills, axis=1), (8, total)).astype(BF)
    width = 128

    def body(step, carry):
        pair = step // (rows // width)
        start = pl.multiple_of(step % (rows // width) * width, width)
        lanes = pl.ds(pl.multiple_of(pair * 128, 128), 128)
        queries = q_ref[pl.ds(start, width), lanes]
        keys = kf[:, lanes]
        mask = dotf(fill8, jnp.ones((8, width), BF), TN) > 0.5
        own = lax.broadcasted_iota(jnp.int32, (total, width), 0) == (
            lax.broadcasted_iota(jnp.int32, (total, width), 1) + start
        )
        allowed = mask | own
        for head in range(2):
            part = jnp.where(low if head == 0 else ~low, keys, jnp.zeros_like(keys))
            scores = jnp.where(allowed, dotf(part, queries, NT), -1e30)
            weights = jnp.exp2(scores - jnp.max(scores, axis=0, keepdims=True))
            weights = weights / jnp.sum(weights, axis=0, keepdims=True)
            first = pl.multiple_of(pair * 128 + head * HEAD, HEAD)
            values = vf[pl.ds(first, HEAD), :]
            att_ref[pl.ds(first, HEAD), pl.ds(start, width)] = dotf(
                values, weights.astype(BF)
            ).astype(BF)
        return carry

    lax.fori_loop(0, HEADS // 2 * (rows // width), body, 0)


def finish_attention(level, chunk_refs, chunk_rows, operands, scratch, fill, fills_far):
    last, gains, kw, vw, q, qp, kp, o_in, k_loc, vt_loc = operands
    att_ref, km_ref, va_ref, o_scr, xbuf, kf, vf = scratch
    rows = km_ref.shape[1]
    normed = norm_rows(last.here[:rows, :], gains.here[level : level + 1, :])
    keys, values_t = project_kv(normed, kw, vw)
    split_keys(keys, km_ref)
    split_values(values_t, fills_far[-1], va_ref)
    peak = jnp.maximum(kp.here[...], head_peak(keys)) * qp.here[...]
    attend(q.here, km_ref, va_ref, o_scr, o_in.here)
    for head in range(HEADS):
        scale = 1.0 / o_scr[head, HEAD : HEAD + 1, :]
        att_ref[head * HEAD : (head + 1) * HEAD, :] = (o_scr[head, :HEAD, :] * scale).astype(BF)
    inside = jnp.max(peak) <= LIMIT2

    @pl.when(jnp.logical_not(inside))
    def _():
        exact_attend(level, q.here, [fill] + fills_far, chunk_refs, chunk_rows, gains,
                     kw, vw, k_loc, vt_loc, att_ref, xbuf, kf, vf)

    return att_ref[...]


def finish0_kernel(counts, *refs):
    n = len(counts)
    chunks = refs[:n]
    (last, fill_ref, far_ref, gains, kw, vw, ow, q, qp, kp, o_in, k_loc, vt_loc, points, tree,
     y_out, x1_out) = refs[n : n + 17]
    scratch = refs[n + 17 :]
    fill = fill_ref.here[...].astype(F32)
    far = far_ref.here[...].astype(F32)
    fills_far, at = [], 0
    for count in counts:
        fills_far.append(far[:, at : at + count])
        at += count
    attended_t = finish_attention(
        0, chunks, counts, (last, gains, kw, vw, q, qp, kp, o_in, k_loc, vt_loc), scratch, fill,
        fills_far)
    x0 = points.here[...].astype(F32) * to_column(fill)
    y = (x0 + dotf(attended_t, ow.here[...], TN)).astype(BF)
    y_out.ref[...] = y
    y_out.flush()
    lanes = lax.broadcasted_iota(jnp.int32, (256, 1024), 1)
    f8 = jnp.broadcast_to(fill, (8, 1024)).astype(BF)
    order = tree.here
    fills = []
    for half in range(2):
        picked = (lanes == order[:, 2 * half : 2 * half + 1]) | (
            lanes == order[:, 2 * half + 1 : 2 * half + 2]
        )
        pool = jnp.where(picked, 0.5, 0.0).astype(BF)
        x1_out.ref[half * 256 : (half + 1) * 256, :] = dotf(pool, y).astype(BF)
        fills.append(jnp.where(dotf(f8, pool, NT)[:1] > 0.25, 1.0, 0.0))
    x1_out.ref[512:, :] = jnp.broadcast_to(jnp.concatenate(fills, axis=1), (16, D)).astype(BF)
    x1_out.flush()


def finish1_kernel(counts, far, last, gains, kw, vw, ow, q, qp, kp, o_in, k_loc, vt_loc, x,
                   y_out, x2_out, *scratch):
    fill = x.here[512:513, :].astype(F32)
    fills_far = [last.here[512:513, :].astype(F32)]
    attended_t = finish_attention(
        1, [far], counts, (last, gains, kw, vw, q, qp, kp, o_in, k_loc, vt_loc), scratch, fill,
        fills_far)
    y = (x.here[:512, :].astype(F32) + dotf(attended_t, ow.here[...], TN)).astype(BF)
    wide = y.astype(F32)
    x2_out.ref[:256, :] = ((wide[:256] + wide[256:]) * 0.5).astype(BF)
    f_next = jnp.maximum(fill[:, :256], fill[:, 256:])
    x2_out.ref[256:, :] = jnp.broadcast_to(
        jnp.concatenate([f_next, f_next], axis=1), (16, D)).astype(BF)
    x2_out.flush()
    y_out.ref[...] = y
    y_out.flush()


def finish2_kernel(counts, far, last, gains, kw, vw, ow, q, qp, kp, o_in, k_loc, vt_loc, x,
                   gm, hw, pw, y1, y0, tree, field, *scratch):
    fill = x.here[256:257, :256].astype(F32)
    fills_far = [last.here[256:257, :256].astype(F32)]
    attended_t = finish_attention(
        2, [far], counts, (last, gains, kw, vw, q, qp, kp, o_in, k_loc, vt_loc), scratch, fill,
        fills_far)
    y2 = (x.here[:256, :].astype(F32) + dotf(attended_t, ow.here[...], TN)).astype(BF)
    normed = norm_rows(y2, gm.here[...])
    hidden = jax.nn.gelu(dotf(normed, hw.here[...]), approximate=True).astype(BF)
    top = (y2.astype(F32) + dotf(hidden, pw.here[...])).astype(BF).astype(F32)
    up = [(y1.here[half * 256 : (half + 1) * 256, :].astype(F32) + top).astype(BF)
          for half in range(2)]
    rows = lax.broadcasted_iota(jnp.int32, (1024, 256), 0)
    total = y0.here[...].astype(F32)
    order = tree.here
    for half in range(2):
        picked = (rows == order[2 * half : 2 * half + 1, :]) | (
            rows == order[2 * half + 1 : 2 * half + 2, :]
        )
        total = total + dotf(jnp.where(picked, 1.0, 0.0).astype(BF), up[half])
    field.ref[...] = total.astype(BF)
    field.flush()


class Piece:
    def __init__(self, copy, ref):
        self.copy, self.ref = copy, ref

    @property
    def here(self):
        if self.copy is not None:
            self.copy.wait()
            self.copy = None
        return self.ref


class Result:
    def __init__(self, ref, copy):
        self.ref, self.copy = ref, copy

    def flush(self):
        self.copy.start()


def call(kernel, outs, args, raw=(), scratch=(), flops=0):
    arrays = [a[0] if isinstance(a, tuple) else a for a in args]
    levels = [a[1] if isinstance(a, tuple) else None for a in args]
    n, m = len(args), len(outs)
    moved = [i for i in range(n) if i not in raw]
    buffers = [
        pltpu.VMEM(a.shape if lv is None else a.shape[1:], a.dtype)
        for i, (a, lv) in enumerate(zip(arrays, levels)) if i not in raw
    ]

    def body(*refs):
        sources, targets = refs[:n], refs[n : n + m]
        held, rest = refs[n + m : n + m + len(moved)], refs[n + m + len(moved) :]
        results, rest = rest[:m], rest[m:]
        sem_in, sem_out, rest = rest[0], rest[1], rest[2:]
        operands = list(sources)
        for slot, i in enumerate(moved):
            source = sources[i] if levels[i] is None else sources[i].at[levels[i]]
            copy = pltpu.make_async_copy(source, held[slot], sem_in.at[slot])
            copy.start()
            operands[i] = Piece(copy, held[slot])
        products = [
            Result(results[i], pltpu.make_async_copy(results[i], targets[i], sem_out.at[i]))
            for i in range(m)
        ]
        kernel(*operands, *products, *rest)
        for operand in operands:
            if isinstance(operand, Piece):
                operand.here
        for product in products:
            product.copy.wait()

    nbytes = sum(a.size * a.dtype.itemsize for a in arrays) + sum(
        a.size * a.dtype.itemsize for a in outs)
    return pl.pallas_call(
        body,
        out_shape=outs,
        in_specs=[ANY] * n,
        out_specs=[ANY] * m,
        scratch_shapes=buffers + [pltpu.VMEM(o.shape, o.dtype) for o in outs]
        + [pltpu.SemaphoreType.DMA((len(moved),)), pltpu.SemaphoreType.DMA((m,))]
        + list(scratch),
        compiler_params=pltpu.CompilerParams(vmem_limit_bytes=VLIMIT),
        cost_estimate=pl.CostEstimate(flops=flops, bytes_accessed=nbytes, transcendentals=0),
    )(*arrays)


def shape(*dims, dtype=BF):
    return jax.ShapeDtypeStruct(dims, dtype)


def local_part(level, x, fill, gains, qw, kw, vw, rows):
    return call(
        functools.partial(local_kernel, level, rows),
        [shape(rows, D), shape(rows, D), shape(D, rows), shape(HEADS, VROWS, rows, dtype=F32),
         shape(16, 128, dtype=F32), shape(16, 128, dtype=F32)],
        [x, fill, gains, (qw, level), (kw, level), (vw, level)],
        scratch=[pltpu.VMEM((HEADS, rows, 128), BF), pltpu.VMEM((HEADS, VROWS, rows), BF)],
        flops=8 * rows * rows * 512 * 2,
    )


def remote_part(level, at, x, fill, gains, kw, vw, q, kp, o, count):
    rows = q.shape[0]
    return call(
        functools.partial(remote_kernel, level, at),
        [shape(HEADS, VROWS, rows, dtype=F32), shape(16, 128, dtype=F32)],
        [x, fill, gains, (kw, level), (vw, level), q, kp, o],
        scratch=[pltpu.VMEM((HEADS, count, 128), BF), pltpu.VMEM((HEADS, VROWS, count), BF)],
        flops=8 * rows * count * 512 * 2,
    )


def finish_part(kernel, counts, chunks, args, outs, rows, raw):
    n = len(counts)
    return call(
        functools.partial(kernel, counts),
        outs,
        list(chunks) + [chunks[-1]] + args,
        raw=set(range(n)) | {n + 1 + i for i in raw},
        scratch=[
            pltpu.VMEM((D, rows), BF),
            pltpu.VMEM((HEADS, counts[-1], 128), BF),
            pltpu.VMEM((HEADS, VROWS, counts[-1]), BF),
            pltpu.VMEM((HEADS, VROWS, rows), F32),
            pltpu.VMEM((max(counts), D), BF),
            pltpu.VMEM((2 * rows, D), BF),
            pltpu.VMEM((D, 2 * rows), BF),
        ],
        flops=8 * rows * counts[-1] * 512 * 2 + 4 * rows * D * D,
    )


def per_device(points, tree_order, present, gain_attn, query_weight, key_weight, value_weight,
               out_weight, gain_mlp, hidden_weight, proj_weight):
    size = lax.axis_size("leaf")

    def trade(value, bit):
        return lax.ppermute(value, "leaf", [(s, s ^ (1 << bit)) for s in range(size)])

    base = size.bit_length() - 1 - 3
    fill0 = present.reshape(1, 1024)
    far_fill = trade(fill0, base)
    counts0 = (384, 256, 256, 128)
    chunks, at = [], 0
    for i, count in enumerate(counts0):
        part = points[at : at + count]
        if i >= 2:
            part, _ = lax.optimization_barrier((part, chunks[i - 2]))
        chunks.append(trade(part, base))
        at += count
    tree4 = tree_order.reshape(256, 4)
    tree_rows = tree4.T

    def kvs(level):
        return [(key_weight, level), (value_weight, level)]

    q, k, vt, o, qp, kp = local_part(0, points, fill0, gain_attn, query_weight, key_weight,
                                     value_weight, 1024)
    at = 0
    for chunk, count in zip(chunks[:-1], counts0[:-1]):
        o, kp = remote_part(0, at, chunk, far_fill, gain_attn, key_weight, value_weight, q, kp, o,
                            count)
        at += count
    y0, x1 = finish_part(
        finish0_kernel, counts0, chunks,
        [fill0, far_fill, gain_attn, *kvs(0), (out_weight, 0), q, qp, kp, o, k, vt, points, tree4],
        [shape(1024, D), shape(528, D)], 1024, raw={10, 11})
    far1 = trade(x1, base + 1)
    q, k, vt, o, qp, kp = local_part(1, x1, fill0, gain_attn, query_weight, key_weight,
                                     value_weight, 512)
    y1, x2 = finish_part(
        finish1_kernel, (512,), [far1],
        [gain_attn, *kvs(1), (out_weight, 1), q, qp, kp, o, k, vt, x1],
        [shape(512, D), shape(272, D)], 512, raw={8, 9})
    far2 = trade(x2, base + 2)
    q, k, vt, o, qp, kp = local_part(2, x2, fill0, gain_attn, query_weight, key_weight,
                                     value_weight, 256)
    (field,) = finish_part(
        finish2_kernel, (256,), [far2],
        [gain_attn, *kvs(2), (out_weight, 2), q, qp, kp, o, k, vt, x2, gain_mlp.reshape(1, D),
         hidden_weight, proj_weight, y1, y0, tree_rows],
        [shape(1024, D)], 256, raw={8, 9})
    return field


def solution(mesh):
    placed = (
        P(("cloud", "leaf"), None),
        P(("cloud", "leaf")),
        P(("cloud", "leaf")),
        P(), P(), P(), P(), P(), P(), P(), P(),
    )
    return jax.shard_map(
        per_device,
        mesh=mesh,
        in_specs=placed,
        out_specs=P(("cloud", "leaf"), None),
        check_vma=False,
    )
```

```python
import functools
import jax
import jax.numpy as jnp
from jax import lax
from jax.experimental import pallas as pl
from jax.experimental.pallas import tpu as pltpu
from jax.sharding import PartitionSpec as P

D = 512
HEAD = 64
HEADS = 8
VROWS = 80
LIMIT2 = 60.0**2
QSCALE = HEAD ** (-0.5)
NT = (((1,), (1,)), ((), ()))
TN = (((0,), (0,)), ((), ()))
BF = jnp.bfloat16
F32 = jnp.float32
ANY = pl.BlockSpec(memory_space=pl.ANY)
VMEM = pl.BlockSpec(memory_space=pltpu.VMEM)
FLAT = 1024 * 512
SENT = (256, 288, 288, 192)
USUAL = sum(SENT[:-1])
EARLY = SENT[0]


def dotf(a, b, dims=(((1,), (0,)), ((), ()))):
    return lax.dot_general(a, b, dims, preferred_element_type=F32)


def norm_rows(values, gain):
    wide = values.astype(F32)
    centre = jnp.mean(wide, axis=-1, keepdims=True)
    wide = wide - centre
    spread = jnp.mean(jnp.square(wide), axis=-1, keepdims=True)
    return (wide * lax.rsqrt(spread + 1e-05) * gain).astype(BF)


def to_column(row):
    eye = lax.broadcasted_iota(jnp.int32, (128, 128), 0) == lax.broadcasted_iota(
        jnp.int32, (128, 128), 1
    )
    parts = []
    for start in range(0, row.shape[1], 128):
        block = jnp.where(eye, row[:, start : start + 128], 0.0)
        parts.append(jnp.sum(block, axis=1, keepdims=True))
    return jnp.concatenate(parts, axis=0)


def head_select():
    lane = lax.broadcasted_iota(jnp.int32, (16, D), 1)
    head = lax.broadcasted_iota(jnp.int32, (16, D), 0)
    return jnp.where(lane // HEAD == head, 1.0, 0.0).astype(BF)


def head_peak(rows):
    wide = rows.astype(F32)
    sums = dotf(head_select(), (wide * wide).astype(BF), NT)
    return jnp.broadcast_to(jnp.max(sums, axis=1, keepdims=True), (16, 128))


def split_keys(keys, km_ref):
    low = lax.broadcasted_iota(jnp.int32, (1, 128), 1) < HEAD
    for pair in range(HEADS // 2):
        part = keys[:, pair * 128 : (pair + 1) * 128]
        km_ref[2 * pair] = jnp.where(low, part, jnp.zeros_like(part))
        km_ref[2 * pair + 1] = jnp.where(low, jnp.zeros_like(part), part)


def split_values(values_t, fill_row, va_ref):
    width = values_t.shape[1]
    fill = fill_row.astype(BF)
    first = lax.broadcasted_iota(jnp.int32, (16, width), 0) == 0
    ones = jnp.where(first, fill_row, 0.0).astype(BF)
    masked = values_t * fill
    for head in range(HEADS):
        va_ref[head, :HEAD, :] = masked[head * HEAD : (head + 1) * HEAD]
        va_ref[head, HEAD:, :] = ones


def attend(q_ref, km_ref, va_ref, o_ref, add_ref):
    count = km_ref.shape[1]
    blocks = [(start, min(256, count - start)) for start in range(0, count, 256)]

    def run(pairs, lanes_of):
        waiting, totals = [], {}

        def drain():
            pair, head, block, scores = waiting.pop(0)
            start, size = block
            weights = jnp.exp(scores).astype(BF)
            part = dotf(va_ref[pair * 2 + head, :, start : start + size], weights)
            total = totals.pop(head, None)
            total = part if total is None else total + part
            if block == blocks[-1]:
                if add_ref is not None:
                    total = total + add_ref[pair * 2 + head]
                o_ref[pair * 2 + head] = total
            else:
                totals[head] = total

        for pair in pairs:
            queries = q_ref[:, lanes_of(pair)]
            for head in range(2):
                for block in blocks:
                    start, size = block
                    keys = km_ref[pair * 2 + head, start : start + size, :]
                    waiting.append((pair, head, block, dotf(keys, queries, NT)))
                    if len(waiting) > 1:
                        drain()
        while waiting:
            drain()

    if q_ref.shape[0] * count <= FLAT:
        run(range(HEADS // 2), lambda pair: slice(pair * 128, (pair + 1) * 128))
        return

    def body(pair, carry):
        run([pair], lambda pair: pl.ds(pl.multiple_of(pair * 128, 128), 128))
        return carry

    lax.fori_loop(0, HEADS // 2, body, 0)


def project_kv(normed, kw, vw):
    keys = dotf(normed, kw.here[...]).astype(BF)
    values_t = dotf(vw.here[...], normed, (((0,), (1,)), ((), ()))).astype(BF)
    return keys, values_t


def front_kernel(points, present, *outs):
    fill = present.here[...].astype(F32)
    upto = lax.broadcasted_iota(jnp.int32, (1024, 1024), 0) <= lax.broadcasted_iota(
        jnp.int32, (1024, 1024), 1
    )
    f8 = jnp.broadcast_to(fill, (8, 1024)).astype(BF)
    rank = dotf(f8, jnp.where(upto, 1.0, 0.0).astype(BF))[:1]
    place = jnp.where(fill > 0.0, rank - 1.0, -1.0).astype(jnp.int32)
    at = 0
    for out, count in zip(outs, SENT):
        rows = lax.broadcasted_iota(jnp.int32, (count, 1024), 0) + at
        pick = jnp.where(rows == place, 1.0, 0.0).astype(BF)
        out.ref[:count, :] = dotf(pick, points.here[...]).astype(BF)
        if out is outs[0]:
            lane = lax.broadcasted_iota(jnp.int32, (16, D), 1)
            line = lax.broadcasted_iota(jnp.int32, (16, D), 0)
            total = jnp.broadcast_to(rank[:, 1023:], (16, D)).astype(jnp.int32)
            out.ref[count:, :] = jnp.where(line * D + lane < total, 1.0, 0.0).astype(BF)
        out.flush()
        at += count


def local_kernel(level, rows, x, fill_src, gains, qw, kw, vw,
                 q, o, qp, kp, km_ref, va_ref):
    normed = norm_rows(x.here[:rows, :], gains.here[level : level + 1, :])
    if level == 0:
        fill = fill_src.here[...].astype(F32)
        normed = normed * to_column(fill).astype(BF)
    else:
        fill = x.here[rows : rows + 1, :rows].astype(F32)
    queries = dotf(normed, qw.here[...]).astype(BF) * QSCALE
    q.ref[...] = queries
    q.flush()
    keys, values_t = project_kv(normed, kw, vw)
    qp.ref[...] = head_peak(queries)
    kp.ref[...] = head_peak(keys)
    qp.flush()
    kp.flush()
    split_keys(keys, km_ref)
    split_values(values_t, fill, va_ref)
    attend(q.ref, km_ref, va_ref, o.ref, None)
    if level == 0:
        for head in range(HEADS):
            o.ref[head, HEAD : HEAD + 1, :] += 1.0 - fill
    else:
        prod = queries.astype(F32) * keys.astype(F32)
        high = prod.astype(BF)
        rest = (prod - high.astype(F32)).astype(BF)
        select = head_select()
        own = jnp.exp(dotf(select, high, NT) + dotf(select, rest, NT))
        own = own * (1.0 - fill)
        for head in range(HEADS):
            weight = own[head : head + 1]
            part = values_t[head * HEAD : (head + 1) * HEAD].astype(F32)
            o.ref[head, :HEAD, :] += part * weight
            o.ref[head, HEAD : HEAD + 1, :] += weight
    o.flush()


def far_fill(packed):
    at = packed.shape[0] - 16
    return jnp.concatenate([packed[at : at + 1, :], packed[at + 1 : at + 2, :]], axis=1).astype(F32)


def remote_kernel(first, gains, kw, vw, q, o_in, kp_in, o, kp, km_ref, va_ref):
    normed = norm_rows(first.here[:EARLY, :], gains.here[0:1, :])
    keys, values_t = project_kv(normed, kw, vw)
    split_keys(keys, km_ref)
    split_values(values_t, far_fill(first.here)[:, :EARLY], va_ref)
    kp.ref[...] = jnp.maximum(kp_in.here[...], head_peak(keys))
    kp.flush()
    attend(q.here, km_ref, va_ref, o.ref, o_in.here)
    o.flush()


def exact_attend(level, q_ref, own, fills, chunks, counts, gains, kw, vw, att_ref, xbuf, kf, vf):
    rows = q_ref.shape[0]
    for side, sources in enumerate(([(own, rows)], list(zip(chunks, counts)))):
        at = 0
        for ref, count in sources:
            pltpu.sync_copy(ref.at[pl.ds(0, count), :], xbuf.at[pl.ds(at, count), :])
            at += count
        for start in range(0, rows, 128):
            normed = norm_rows(xbuf[start : start + 128, :], gains.here[level : level + 1, :])
            if level == 0 and side == 0:
                normed = normed * to_column(fills[0][:, start : start + 128]).astype(BF)
            keys, values_t = project_kv(normed, kw, vw)
            base = side * rows + start
            kf[base : base + 128, :] = keys
            vf[:, base : base + 128] = values_t
    total = 2 * rows
    low = lax.broadcasted_iota(jnp.int32, (1, 128), 1) < HEAD
    fill8 = jnp.broadcast_to(jnp.concatenate(fills, axis=1), (8, total)).astype(BF)
    width = 128

    def body(step, carry):
        pair = step // (rows // width)
        start = pl.multiple_of(step % (rows // width) * width, width)
        lanes = pl.ds(pl.multiple_of(pair * 128, 128), 128)
        queries = q_ref[pl.ds(start, width), lanes]
        keys = kf[:, lanes]
        mask = dotf(fill8, jnp.ones((8, width), BF), TN) > 0.5
        own = lax.broadcasted_iota(jnp.int32, (total, width), 0) == (
            lax.broadcasted_iota(jnp.int32, (total, width), 1) + start
        )
        allowed = mask | own
        for head in range(2):
            part = jnp.where(low if head == 0 else ~low, keys, jnp.zeros_like(keys))
            scores = jnp.where(allowed, dotf(part, queries, NT), -1e30)
            weights = jnp.exp(scores - jnp.max(scores, axis=0, keepdims=True))
            weights = weights / jnp.sum(weights, axis=0, keepdims=True)
            first = pl.multiple_of(pair * 128 + head * HEAD, HEAD)
            values = vf[pl.ds(first, HEAD), :]
            att_ref[pl.ds(first, HEAD), pl.ds(start, width)] = dotf(
                values, weights.astype(BF)
            ).astype(BF)
        return carry

    lax.fori_loop(0, HEADS // 2 * (rows // width), body, 0)


def finish_attention(level, far, chunk_refs, counts, operands, scratch, fill, fill_far, rest=None):
    gains, kw, vw, q, qp, kp, o, own = operands
    att_ref, km_ref, va_ref, xbuf, kf, vf = scratch[:6]
    gain = gains.here[level : level + 1, :]
    count = km_ref.shape[1]
    begin = 0 if rest is None else EARLY
    usual = begin + count
    normed = [norm_rows(x.here[:count, :], gain) for x, count in zip(far, counts)]
    normed = jnp.concatenate(normed, axis=0) if len(normed) > 1 else normed[0]
    keys, values_t = project_kv(normed, kw, vw)
    split_keys(keys, km_ref)
    split_values(values_t, fill_far[:, begin:usual], va_ref)
    peak = jnp.maximum(kp.here[...], head_peak(keys)) * qp.here[...]
    attend(q.here, km_ref, va_ref, o.here, o.here)
    if rest is not None:
        rest_km, rest_va, rest_peak = scratch[6:]
        rest_peak[...] = jnp.zeros_like(rest_peak)

        @pl.when(jnp.max(fill_far[:, usual:]) > 0.0)
        def _():
            keys, values_t = project_kv(norm_rows(rest.here[...], gain), kw, vw)
            split_keys(keys, rest_km)
            split_values(values_t, fill_far[:, usual:], rest_va)
            rest_peak[...] = head_peak(keys)
            attend(q.here, rest_km, rest_va, o.here, o.here)

        peak = jnp.maximum(peak, rest_peak[...] * qp.here[...])
    for head in range(HEADS):
        scale = 1.0 / o.here[head, HEAD : HEAD + 1, :]
        att_ref[head * HEAD : (head + 1) * HEAD, :] = (o.here[head, :HEAD, :] * scale).astype(BF)
    inside = jnp.max(peak) <= LIMIT2

    @pl.when(jnp.logical_not(inside))
    def _():
        exact_attend(level, q.here, own.here, [fill, fill_far], chunk_refs,
                     counts if rest is None else SENT, gains, kw, vw, att_ref, xbuf, kf, vf)

    return att_ref[...]


def finish0_kernel(*refs):
    chunks = refs[: len(SENT)]
    (second, third, packed, rest, fill_ref, gains, kw, vw, q, o, ow, qp, kp, points, tree,
     y_out, x1_out) = refs[len(SENT) : len(SENT) + 17]
    scratch = refs[len(SENT) + 17 :]
    rest.here
    fill = fill_ref.here[...].astype(F32)
    points.here
    attended_t = finish_attention(
        0, [second, third], chunks, SENT[1:3], (gains, kw, vw, q, qp, kp, o, points), scratch,
        fill, far_fill(packed.here), rest)
    x0 = points.here[...].astype(F32) * to_column(fill)
    y = (x0 + dotf(attended_t, ow.here[...], TN)).astype(BF)
    y_out.ref[...] = y
    y_out.flush()
    lanes = lax.broadcasted_iota(jnp.int32, (256, 1024), 1)
    f8 = jnp.broadcast_to(fill, (8, 1024)).astype(BF)
    order = tree.here
    fills = []
    for half in range(2):
        picked = (lanes == order[:, 2 * half : 2 * half + 1]) | (
            lanes == order[:, 2 * half + 1 : 2 * half + 2]
        )
        pool = jnp.where(picked, 0.5, 0.0).astype(BF)
        x1_out.ref[half * 256 : (half + 1) * 256, :] = dotf(pool, y).astype(BF)
        fills.append(jnp.where(dotf(f8, pool, NT)[:1] > 0.25, 1.0, 0.0))
    x1_out.ref[512:, :] = jnp.broadcast_to(jnp.concatenate(fills, axis=1), (16, D)).astype(BF)
    x1_out.flush()


def finish1_kernel(far_hbm, last, gains, kw, vw, ow, q, qp, kp, o_in, x, y_out, x2_out, *scratch):
    fill = x.here[512:513, :].astype(F32)
    attended_t = finish_attention(
        1, [last], [far_hbm], (512,), (gains, kw, vw, q, qp, kp, o_in, x), scratch, fill,
        last.here[512:513, :].astype(F32))
    y = (x.here[:512, :].astype(F32) + dotf(attended_t, ow.here[...], TN)).astype(BF)
    wide = y.astype(F32)
    x2_out.ref[:256, :] = ((wide[:256] + wide[256:]) * 0.5).astype(BF)
    f_next = jnp.maximum(fill[:, :256], fill[:, 256:])
    x2_out.ref[256:, :] = jnp.broadcast_to(
        jnp.concatenate([f_next, f_next], axis=1), (16, D)).astype(BF)
    x2_out.flush()
    y_out.ref[...] = y
    y_out.flush()


def finish2_kernel(far_hbm, last, gains, kw, vw, q, o_in, qp, kp, x, ow, gm, hw, pw, y1, y0, tree,
                   field, *scratch):
    fill = x.here[256:257, :256].astype(F32)
    attended_t = finish_attention(
        2, [last], [far_hbm], (256,), (gains, kw, vw, q, qp, kp, o_in, x), scratch, fill,
        last.here[256:257, :256].astype(F32))
    y2 = (x.here[:256, :].astype(F32) + dotf(attended_t, ow.here[...], TN)).astype(BF)
    normed = norm_rows(y2, gm.here[...])
    hidden = jax.nn.gelu(dotf(normed, hw.here[...]), approximate=True).astype(BF)
    top = (y2.astype(F32) + dotf(hidden, pw.here[...])).astype(BF).astype(F32)
    up = [(y1.here[half * 256 : (half + 1) * 256, :].astype(F32) + top).astype(BF)
          for half in range(2)]
    rows = lax.broadcasted_iota(jnp.int32, (1024, 256), 0)
    total = y0.here[...].astype(F32)
    order = tree.here
    for half in range(2):
        picked = (rows == order[2 * half : 2 * half + 1, :]) | (
            rows == order[2 * half + 1 : 2 * half + 2, :]
        )
        total = total + dotf(jnp.where(picked, 1.0, 0.0).astype(BF), up[half])
    field.ref[...] = total.astype(BF)
    field.flush()


class Here:
    def __init__(self, ref, copy=None):
        self.here = self.ref = ref
        self.copy = copy

    def flush(self):
        if self.copy is not None:
            self.copy.start()


class Piece:
    def __init__(self, copy, ref):
        self.copy, self.ref = copy, ref

    @property
    def here(self):
        if self.copy is not None:
            self.copy.wait()
            self.copy = None
        return self.ref


def call(kernel, outs, args, raw=(), scratch=(), flops=0, limit=16, manual=False):
    arrays = [a[0] if isinstance(a, tuple) else a for a in args]
    n, m = len(args), len(outs)
    moved = [i for i in range(n) if isinstance(args[i], tuple) or (manual and i not in raw)]
    level = [args[i][1] if isinstance(args[i], tuple) else None for i in range(n)]
    buffers = [
        pltpu.VMEM(arrays[i].shape if level[i] is None else arrays[i].shape[1:], arrays[i].dtype)
        for i in moved
    ]
    sems = [pltpu.SemaphoreType.DMA((len(moved),))] if moved else []
    if manual:
        buffers = [pltpu.VMEM(o.shape, o.dtype) for o in outs] + buffers
        sems.append(pltpu.SemaphoreType.DMA((m,)))

    def body(*refs):
        sources, targets, rest = refs[:n], refs[n : n + m], list(refs[n + m :])
        results = [Here(t) for t in targets]
        if manual:
            held, rest = rest[:m], rest[m:]
        slots, rest = rest[: len(moved)], rest[len(moved) :]
        operands = [s if i in raw else Here(s) for i, s in enumerate(sources)]
        if moved:
            sem = rest.pop(0)
        if manual:
            out_sem = rest.pop(0)
            results = [
                Here(h, pltpu.make_async_copy(h, targets[i], out_sem.at[i]))
                for i, h in enumerate(held)
            ]
        for slot, i in enumerate(moved):
            source = sources[i] if level[i] is None else sources[i].at[level[i]]
            copy = pltpu.make_async_copy(source, slots[slot], sem.at[slot])
            copy.start()
            operands[i] = Piece(copy, slots[slot])
        kernel(*operands, *results, *rest)
        for i in moved:
            operands[i].here
        if manual:
            for result in results:
                result.copy.wait()

    nbytes = sum(a.size * a.dtype.itemsize for a in arrays) + sum(
        a.size * a.dtype.itemsize for a in outs)
    return pl.pallas_call(
        body,
        out_shape=outs,
        in_specs=[ANY if manual or i in raw or i in moved else VMEM for i in range(n)],
        out_specs=[ANY if manual else VMEM] * m,
        scratch_shapes=buffers + sems + list(scratch),
        compiler_params=pltpu.CompilerParams(vmem_limit_bytes=(64 if manual else limit) * 2**20),
        cost_estimate=pl.CostEstimate(flops=flops, bytes_accessed=nbytes, transcendentals=0),
    )(*arrays)


def shape(*dims, dtype=BF):
    return jax.ShapeDtypeStruct(dims, dtype)


def local_part(level, x, fill, gains, qw, kw, vw, rows, manual):
    return call(
        functools.partial(local_kernel, level, rows),
        [shape(rows, D), shape(HEADS, VROWS, rows, dtype=F32),
         shape(16, 128, dtype=F32), shape(16, 128, dtype=F32)],
        [x, fill, gains, (qw, level), (kw, level), (vw, level)],
        scratch=[pltpu.VMEM((HEADS, rows, 128), BF), pltpu.VMEM((HEADS, VROWS, rows), BF)],
        flops=8 * rows * rows * 512 * 2,
        manual=manual,
    )


def finish_part(kernel, args, raw, outs, rows, count, manual, extra=()):
    return call(
        kernel,
        outs,
        args,
        raw=set(range(raw)),
        scratch=[
            pltpu.VMEM((D, rows), BF),
            pltpu.VMEM((HEADS, count, 128), BF),
            pltpu.VMEM((HEADS, VROWS, count), BF),
            pltpu.VMEM((rows, D), BF),
            pltpu.VMEM((2 * rows, D), BF),
            pltpu.VMEM((D, 2 * rows), BF),
            *extra,
        ],
        flops=8 * rows * count * 512 * 2 + 4 * rows * D * D,
        manual=manual,
    )


def per_device(points, tree_order, present, gain_attn, query_weight, key_weight, value_weight,
               out_weight, gain_mlp, hidden_weight, proj_weight):
    size = lax.axis_size("leaf")

    def trade(value, bit):
        return lax.ppermute(value, "leaf", [(s, s ^ (1 << bit)) for s in range(size)])

    base = size.bit_length() - 1 - 3
    fill0 = present.reshape(1, 1024)
    parts = call(
        front_kernel,
        [shape(count + (16 if i == 0 else 0), D) for i, count in enumerate(SENT)],
        [points, fill0], flops=10**9, manual=True)
    chunks = [trade(part, base) for part in parts[:-1]]
    tree4 = tree_order.reshape(256, 4)
    tree_rows = tree4.T

    def kvs(level):
        return [(key_weight, level), (value_weight, level)]

    q, o, qp, kp = local_part(0, points, fill0, gain_attn, query_weight, key_weight,
                              value_weight, 1024, True)
    line, lane = SENT[0] + USUAL // D, USUAL % D
    over = jnp.maximum(parts[0][line, lane], chunks[0][line, lane]) > 0
    over, left, q, tree_rows = lax.optimization_barrier((over, parts[-1], q, tree_rows))
    rest = lax.cond(over, lambda left: trade(left, base), lambda left: left, left)
    rest, o = lax.optimization_barrier((rest, o))
    o, kp = call(
        remote_kernel, [shape(HEADS, VROWS, 1024, dtype=F32), shape(16, 128, dtype=F32)],
        [chunks[0], gain_attn, *kvs(0), q, o, kp],
        scratch=[pltpu.VMEM((HEADS, EARLY, 128), BF), pltpu.VMEM((HEADS, VROWS, EARLY), BF)],
        flops=10**10, manual=True)
    chunks.append(rest)
    y0, x1 = finish_part(
        finish0_kernel,
        [*chunks, *chunks[1:3], chunks[0], chunks[3], fill0, gain_attn, *kvs(0), q, o, (out_weight, 0), qp, kp, points,
         tree4],
        len(SENT), [shape(1024, D), shape(528, D)], 1024, USUAL - EARLY, True,
        extra=[pltpu.VMEM((HEADS, SENT[-1], 128), BF), pltpu.VMEM((HEADS, VROWS, SENT[-1]), BF),
               pltpu.VMEM((16, 128), F32)])
    far1 = trade(x1, base + 1)
    q, o, qp, kp = local_part(1, x1, fill0, gain_attn, query_weight, key_weight, value_weight,
                              512, False)
    y1, x2 = finish_part(
        finish1_kernel,
        [far1, far1, gain_attn, *kvs(1), (out_weight, 1), q, qp, kp, o, x1],
        1, [shape(512, D), shape(272, D)], 512, 512, False)
    far2 = trade(x2, base + 2)
    q, o, qp, kp = local_part(2, x2, fill0, gain_attn, query_weight, key_weight, value_weight,
                              256, True)
    (field,) = finish_part(
        finish2_kernel,
        [far2, far2, gain_attn, *kvs(2), q, o, qp, kp, x2, (out_weight, 2),
         gain_mlp.reshape(1, D), (hidden_weight, None), (proj_weight, None), y1, y0, tree_rows],
        1, [shape(1024, D)], 256, 256, True)
    return field


def solution(mesh):
    placed = (
        P(("cloud", "leaf"), None),
        P(("cloud", "leaf")),
        P(("cloud", "leaf")),
        P(), P(), P(), P(), P(), P(), P(), P(),
    )
    return jax.shard_map(
        per_device,
        mesh=mesh,
        in_specs=placed,
        out_specs=P(("cloud", "leaf"), None),
        check_vma=False,
    )
```

```python
import functools
import jax
import jax.numpy as jnp
from jax import lax
from jax.experimental import pallas as pl
from jax.experimental.pallas import tpu as pltpu
from jax.sharding import PartitionSpec as P

D = 512
HEAD = 64
HEADS = 8
VROWS = 80
LIMIT2 = 60.0**2
QSCALE = HEAD ** (-0.5)
NT = (((1,), (1,)), ((), ()))
TN = (((0,), (0,)), ((), ()))
BF = jnp.bfloat16
F32 = jnp.float32
ANY = pl.BlockSpec(memory_space=pl.ANY)
VMEM = pl.BlockSpec(memory_space=pltpu.VMEM)
FLAT = 1024 * 576
SENT = (256, 288, 288, 192)
USUAL = sum(SENT[:-1])
EARLY = SENT[0]


def dotf(a, b, dims=(((1,), (0,)), ((), ()))):
    return lax.dot_general(a, b, dims, preferred_element_type=F32)


def norm_rows(values, gain):
    wide = values.astype(F32)
    centre = jnp.mean(wide, axis=-1, keepdims=True)
    wide = wide - centre
    spread = jnp.mean(jnp.square(wide), axis=-1, keepdims=True)
    return (wide * lax.rsqrt(spread + 1e-05) * gain).astype(BF)


def to_column(row):
    eye = lax.broadcasted_iota(jnp.int32, (128, 128), 0) == lax.broadcasted_iota(
        jnp.int32, (128, 128), 1
    )
    parts = []
    for start in range(0, row.shape[1], 128):
        block = jnp.where(eye, row[:, start : start + 128], 0.0)
        parts.append(jnp.sum(block, axis=1, keepdims=True))
    return jnp.concatenate(parts, axis=0)


def head_select():
    lane = lax.broadcasted_iota(jnp.int32, (16, D), 1)
    head = lax.broadcasted_iota(jnp.int32, (16, D), 0)
    return jnp.where(lane // HEAD == head, 1.0, 0.0).astype(BF)


def head_peak(rows):
    wide = rows.astype(F32)
    sums = dotf(head_select(), (wide * wide).astype(BF), NT)
    return jnp.broadcast_to(jnp.max(sums, axis=1, keepdims=True), (16, 128))


def split_queries(queries, q_ref):
    low = lax.broadcasted_iota(jnp.int32, (1, 128), 1) < HEAD
    for pair in range(HEADS // 2):
        part = queries[:, pair * 128 : (pair + 1) * 128]
        q_ref[2 * pair] = jnp.where(low, part, jnp.zeros_like(part))
        q_ref[2 * pair + 1] = jnp.where(low, jnp.zeros_like(part), part)


def fill_rows(fill_row):
    first = lax.broadcasted_iota(jnp.int32, (16, fill_row.shape[1]), 0) == 0
    return jnp.where(first, fill_row, 0.0).astype(BF)


def attend(q_ref, k_ref, vt_ref, ones_ref, o_ref, add_ref):
    count = k_ref.shape[0]
    blocks = [(start, min(256, count - start)) for start in range(0, count, 256)]
    depth = 2 if q_ref.shape[1] > 256 else 3

    def run(pairs, columns):
        waiting, totals = [], {}

        def drain():
            pair, head, block, scores = waiting.pop(0)
            start, size = block
            weights = jnp.exp(scores).astype(BF)
            keys = slice(start, start + size)
            values = vt_ref[columns(2 * pair + head, HEAD), keys]
            part = dotf(jnp.concatenate([values, ones_ref[:, keys]], axis=0), weights)
            total = totals.pop(head, None)
            total = part if total is None else total + part
            if block == blocks[-1]:
                if add_ref is not None:
                    total = total + add_ref[pair * 2 + head]
                o_ref[pair * 2 + head] = total
            else:
                totals[head] = total

        for pair in pairs:
            for head in range(2):
                queries = q_ref[2 * pair + head]
                for block in blocks:
                    start, size = block
                    keys = k_ref[start : start + size, columns(pair, 128)]
                    waiting.append((pair, head, block, dotf(keys, queries, NT)))
                    if len(waiting) > depth:
                        drain()
        while waiting:
            drain()

    if q_ref.shape[1] * count <= FLAT:
        run(range(HEADS // 2), lambda at, size: slice(at * size, (at + 1) * size))
        return

    def body(pair, carry):
        run([pair], lambda at, size: pl.ds(pl.multiple_of(at * size, size), size))
        return carry

    lax.fori_loop(0, HEADS // 2, body, 0)


def project_kv(normed, kw, vw, fill_row=None):
    keys = dotf(normed, kw.here[...]).astype(BF)
    values_t = dotf(vw.here[...], normed, (((0,), (1,)), ((), ())))
    if fill_row is not None:
        values_t = values_t * fill_row
    return keys, values_t.astype(BF)


def front_kernel(first, points, present, *outs):
    fill = present.here[...].astype(F32)
    upto = lax.broadcasted_iota(jnp.int32, (1024, 1024), 0) <= lax.broadcasted_iota(
        jnp.int32, (1024, 1024), 1
    )
    f8 = jnp.broadcast_to(fill, (8, 1024)).astype(BF)
    rank = dotf(f8, jnp.where(upto, 1.0, 0.0).astype(BF))[:1]
    place = jnp.where(fill > 0.0, rank - 1.0, -1.0).astype(jnp.int32)
    at = sum(SENT[:first])
    for out, count in zip(outs, SENT[first:]):
        rows = lax.broadcasted_iota(jnp.int32, (count, 1024), 0) + at
        pick = jnp.where(rows == place, 1.0, 0.0).astype(BF)
        out.ref[:count, :] = dotf(pick, points.here[...]).astype(BF)
        if at == 0:
            lane = lax.broadcasted_iota(jnp.int32, (16, D), 1)
            line = lax.broadcasted_iota(jnp.int32, (16, D), 0)
            total = jnp.broadcast_to(rank[:, 1023:], (16, D)).astype(jnp.int32)
            out.ref[count:, :] = jnp.where(line * D + lane < total, 1.0, 0.0).astype(BF)
        out.flush()
        at += count


def local_kernel(level, rows, x, fill_src, gains, qw, kw, vw,
                 q, o, qp, kp, k_ref, vt_ref, ones_ref):
    normed = norm_rows(x.here[:rows, :], gains.here[level : level + 1, :])
    if level == 0:
        fill = fill_src.here[...].astype(F32)
        normed = normed * to_column(fill).astype(BF)
    else:
        fill = x.here[rows : rows + 1, :rows].astype(F32)
    queries = dotf(normed, qw.here[...]).astype(BF) * QSCALE
    split_queries(queries, q.ref)
    q.flush()
    keys, values_t = project_kv(normed, kw, vw)
    qp.ref[...] = head_peak(queries)
    kp.ref[...] = head_peak(keys)
    qp.flush()
    kp.flush()
    k_ref[...] = keys
    vt_ref[...] = (values_t.astype(F32) * fill).astype(BF)
    ones_ref[...] = fill_rows(fill)
    attend(q.ref, k_ref, vt_ref, ones_ref, o.ref, None)
    if level == 0:
        for head in range(HEADS):
            o.ref[head, HEAD : HEAD + 1, :] += 1.0 - fill
    else:
        prod = queries.astype(F32) * keys.astype(F32)
        high = prod.astype(BF)
        rest = (prod - high.astype(F32)).astype(BF)
        select = head_select()
        own = jnp.exp(dotf(select, high, NT) + dotf(select, rest, NT))
        own = own * (1.0 - fill)
        for head in range(HEADS):
            weight = own[head : head + 1]
            part = values_t[head * HEAD : (head + 1) * HEAD].astype(F32)
            o.ref[head, :HEAD, :] += part * weight
            o.ref[head, HEAD : HEAD + 1, :] += weight
    o.flush()


def far_fill(packed):
    at = packed.shape[0] - 16
    return jnp.concatenate([packed[at : at + 1, :], packed[at + 1 : at + 2, :]], axis=1).astype(F32)


def remote_kernel(first, gains, kw, vw, q, o_in, kp_in, o, kp, k_ref, vt_ref, ones_ref):
    normed = norm_rows(first.here[:EARLY, :], gains.here[0:1, :])
    fill = far_fill(first.here)[:, :EARLY]
    keys, values_t = project_kv(normed, kw, vw, fill)
    k_ref[...] = keys
    vt_ref[...] = values_t
    ones_ref[...] = fill_rows(fill)
    kp.ref[...] = jnp.maximum(kp_in.here[...], head_peak(keys))
    kp.flush()
    attend(q.here, k_ref, vt_ref, ones_ref, o.ref, o_in.here)
    o.flush()


def exact_attend(level, q_ref, own, fills, chunks, counts, gains, kw, vw, att_ref, xbuf, kf, vf):
    rows = q_ref.shape[1]
    for side, sources in enumerate(([(own, rows)], list(zip(chunks, counts)))):
        at = 0
        for ref, count in sources:
            pltpu.sync_copy(ref.at[pl.ds(0, count), :], xbuf.at[pl.ds(at, count), :])
            at += count
        for start in range(0, rows, 128):
            normed = norm_rows(xbuf[start : start + 128, :], gains.here[level : level + 1, :])
            if level == 0 and side == 0:
                normed = normed * to_column(fills[0][:, start : start + 128]).astype(BF)
            keys, values_t = project_kv(normed, kw, vw)
            base = side * rows + start
            kf[base : base + 128, :] = keys
            vf[:, base : base + 128] = values_t
    total = 2 * rows
    fill8 = jnp.broadcast_to(jnp.concatenate(fills, axis=1), (8, total)).astype(BF)
    width = 128

    def body(step, carry):
        pair = step // (rows // width)
        start = pl.multiple_of(step % (rows // width) * width, width)
        lanes = pl.ds(pl.multiple_of(pair * 128, 128), 128)
        keys = kf[:, lanes]
        mask = dotf(fill8, jnp.ones((8, width), BF), TN) > 0.5
        own = lax.broadcasted_iota(jnp.int32, (total, width), 0) == (
            lax.broadcasted_iota(jnp.int32, (total, width), 1) + start
        )
        allowed = mask | own
        for head in range(2):
            queries = q_ref[2 * pair + head, pl.ds(start, width), :]
            scores = jnp.where(allowed, dotf(keys, queries, NT), -1e30)
            weights = jnp.exp(scores - jnp.max(scores, axis=0, keepdims=True))
            weights = weights / jnp.sum(weights, axis=0, keepdims=True)
            first = pl.multiple_of(pair * 128 + head * HEAD, HEAD)
            values = vf[pl.ds(first, HEAD), :]
            att_ref[pl.ds(first, HEAD), pl.ds(start, width)] = dotf(
                values, weights.astype(BF)
            ).astype(BF)
        return carry

    lax.fori_loop(0, HEADS // 2 * (rows // width), body, 0)


def finish_attention(level, far, chunk_refs, counts, operands, scratch, fill, fill_far, rest=None):
    gains, kw, vw, q, qp, kp, o, own = operands
    att_ref, k_ref, vt_ref, ones_ref, xbuf, kf, vf = scratch[:7]
    gain = gains.here[level : level + 1, :]
    begin = 0 if rest is None else EARLY
    usual = begin + k_ref.shape[0]
    normed = [norm_rows(x.here[:count, :], gain) for x, count in zip(far, counts)]
    normed = jnp.concatenate(normed, axis=0) if len(normed) > 1 else normed[0]
    keys, values_t = project_kv(normed, kw, vw, fill_far[:, begin:usual])
    k_ref[...] = keys
    vt_ref[...] = values_t
    ones_ref[...] = fill_rows(fill_far[:, begin:usual])
    attend(q.here, k_ref, vt_ref, ones_ref, o.here, o.here)
    peak = jnp.maximum(kp.here[...], head_peak(keys)) * qp.here[...]
    own.here
    if rest is not None:
        rest_k, rest_vt, rest_ones, rest_peak = scratch[7:]
        rest_peak[...] = jnp.zeros_like(rest_peak)
        rest.here

        @pl.when(jnp.max(fill_far[:, usual:]) > 0.0)
        def _():
            keys, values_t = project_kv(
                norm_rows(rest.here[...], gain), kw, vw, fill_far[:, usual:])
            rest_k[...] = keys
            rest_vt[...] = values_t
            rest_ones[...] = fill_rows(fill_far[:, usual:])
            rest_peak[...] = head_peak(keys)
            attend(q.here, rest_k, rest_vt, rest_ones, o.here, o.here)

        peak = jnp.maximum(peak, rest_peak[...] * qp.here[...])
    for head in range(HEADS):
        scale = 1.0 / o.here[head, HEAD : HEAD + 1, :]
        att_ref[head * HEAD : (head + 1) * HEAD, :] = (o.here[head, :HEAD, :] * scale).astype(BF)
    inside = jnp.max(peak) <= LIMIT2

    @pl.when(jnp.logical_not(inside))
    def _():
        exact_attend(level, q.here, own.here, [fill, fill_far], chunk_refs,
                     counts if rest is None else SENT, gains, kw, vw, att_ref, xbuf, kf, vf)

    return att_ref[...]


def finish0_kernel(*refs):
    chunks = refs[: len(SENT)]
    (packed, second, third, fill_ref, gains, kw, vw, q, o, qp, kp, ow, points, tree, rest,
     y_out, x1_out) = refs[len(SENT) : len(SENT) + 17]
    scratch = refs[len(SENT) + 17 :]
    fill = fill_ref.here[...].astype(F32)
    attended_t = finish_attention(
        0, [second, third], chunks, SENT[1:3], (gains, kw, vw, q, qp, kp, o, points), scratch,
        fill, far_fill(packed.here), rest)
    x0 = points.here[...].astype(F32) * to_column(fill)
    y = (x0 + dotf(attended_t, ow.here[...], TN)).astype(BF)
    y_out.ref[...] = y
    y_out.flush()
    lanes = lax.broadcasted_iota(jnp.int32, (256, 1024), 1)
    f8 = jnp.broadcast_to(fill, (8, 1024)).astype(BF)
    order = tree.here
    fills = []
    for half in range(2):
        picked = (lanes == order[:, 2 * half : 2 * half + 1]) | (
            lanes == order[:, 2 * half + 1 : 2 * half + 2]
        )
        pool = jnp.where(picked, 0.5, 0.0).astype(BF)
        x1_out.ref[half * 256 : (half + 1) * 256, :] = dotf(pool, y).astype(BF)
        fills.append(jnp.where(dotf(f8, pool, NT)[:1] > 0.25, 1.0, 0.0))
    x1_out.ref[512:, :] = jnp.broadcast_to(jnp.concatenate(fills, axis=1), (16, D)).astype(BF)
    x1_out.flush()


def finish1_kernel(far_hbm, last, gains, kw, vw, q, o_in, qp, kp, x, ow, y_out, x2_out, *scratch):
    fill = x.here[512:513, :].astype(F32)
    attended_t = finish_attention(
        1, [last], [far_hbm], (512,), (gains, kw, vw, q, qp, kp, o_in, x), scratch, fill,
        last.here[512:513, :].astype(F32))
    y = (x.here[:512, :].astype(F32) + dotf(attended_t, ow.here[...], TN)).astype(BF)
    wide = y.astype(F32)
    x2_out.ref[:256, :] = ((wide[:256] + wide[256:]) * 0.5).astype(BF)
    f_next = jnp.maximum(fill[:, :256], fill[:, 256:])
    x2_out.ref[256:, :] = jnp.broadcast_to(
        jnp.concatenate([f_next, f_next], axis=1), (16, D)).astype(BF)
    x2_out.flush()
    y_out.ref[...] = y
    y_out.flush()


def finish2_kernel(far_hbm, last, gains, kw, vw, q, o_in, qp, kp, x, ow, gm, hw, pw, y1, y0, tree,
                   field, *scratch):
    fill = x.here[256:257, :256].astype(F32)
    attended_t = finish_attention(
        2, [last], [far_hbm], (256,), (gains, kw, vw, q, qp, kp, o_in, x), scratch, fill,
        last.here[256:257, :256].astype(F32))
    y2 = (x.here[:256, :].astype(F32) + dotf(attended_t, ow.here[...], TN)).astype(BF)
    normed = norm_rows(y2, gm.here[...])
    hw.here, pw.here
    total = y2.astype(F32)
    before = None
    for start in range(0, 2048 + 512, 512):
        if start < 2048:
            now = dotf(normed, hw.here[:, start : start + 512])
        if before is not None:
            hidden = jax.nn.gelu(before, approximate=True).astype(BF)
            total = total + dotf(hidden, pw.here[start - 512 : start, :])
        before = now
    top = total.astype(BF).astype(F32)
    up = [(y1.here[half * 256 : (half + 1) * 256, :].astype(F32) + top).astype(BF)
          for half in range(2)]
    order = tree.here
    for side, out in enumerate(field.parts(4)):
        rows = lax.broadcasted_iota(jnp.int32, (256, 256), 0) + 256 * side
        total = y0.here[256 * side : 256 * (side + 1), :].astype(F32)
        for half in range(2):
            picked = (rows == order[2 * half : 2 * half + 1, :]) | (
                rows == order[2 * half + 1 : 2 * half + 2, :]
            )
            total = total + dotf(jnp.where(picked, 1.0, 0.0).astype(BF), up[half])
        field.ref[256 * side : 256 * (side + 1), :] = total.astype(BF)
        out.start()


class Here:
    def __init__(self, ref, copy=None):
        self.here = self.ref = ref
        self.copy = copy

    def flush(self):
        if self.copy is not None:
            self.copy.start()

    def parts(self, count):
        rows = self.ref.shape[0] // count
        source, target, sem = self.ends
        return [
            pltpu.make_async_copy(
                source.at[pl.ds(i * rows, rows), :], target.at[pl.ds(i * rows, rows), :], sem)
            for i in range(count)
        ]


class Piece:
    def __init__(self, copy, ref):
        self.copy, self.ref = copy, ref

    @property
    def here(self):
        if self.copy is not None:
            self.copy.wait()
            self.copy = None
        return self.ref


def call(kernel, outs, args, raw=(), scratch=(), flops=0, limit=16, manual=False, away=()):
    arrays = [a[0] if isinstance(a, tuple) else a for a in args]
    n, m = len(args), len(outs)
    moved = [i for i in range(n) if isinstance(args[i], tuple) or (manual and i not in raw)]
    level = [args[i][1] if isinstance(args[i], tuple) else None for i in range(n)]
    buffers = [
        pltpu.VMEM(arrays[i].shape if level[i] is None else arrays[i].shape[1:], arrays[i].dtype)
        for i in moved
    ]
    away = list(range(m)) if manual else sorted(away)
    sems = [pltpu.SemaphoreType.DMA((len(moved),))] if moved else []
    if away:
        buffers = [pltpu.VMEM(outs[i].shape, outs[i].dtype) for i in away] + buffers
        sems.append(pltpu.SemaphoreType.DMA((m,)))

    def body(*refs):
        sources, targets, rest = refs[:n], refs[n : n + m], list(refs[n + m :])
        results = [Here(t) for t in targets]
        held, rest = rest[: len(away)], rest[len(away) :]
        slots, rest = rest[: len(moved)], rest[len(moved) :]
        operands = [s if i in raw else Here(s) for i, s in enumerate(sources)]
        if moved:
            sem = rest.pop(0)
        if away:
            out_sem = rest.pop(0)
        for i, h in zip(away, held):
            results[i] = Here(h, pltpu.make_async_copy(h, targets[i], out_sem.at[i]))
            results[i].ends = (h, targets[i], out_sem.at[i])
        for slot, i in enumerate(moved):
            source = sources[i] if level[i] is None else sources[i].at[level[i]]
            copy = pltpu.make_async_copy(source, slots[slot], sem.at[slot])
            copy.start()
            operands[i] = Piece(copy, slots[slot])
        kernel(*operands, *results, *rest)
        for i in moved:
            operands[i].here
        for i in away:
            results[i].copy.wait()

    nbytes = sum(a.size * a.dtype.itemsize for a in arrays) + sum(
        a.size * a.dtype.itemsize for a in outs)
    return pl.pallas_call(
        body,
        out_shape=outs,
        in_specs=[ANY if manual or i in raw or i in moved else VMEM for i in range(n)],
        out_specs=[ANY if i in away else VMEM for i in range(m)],
        scratch_shapes=buffers + sems + list(scratch),
        compiler_params=pltpu.CompilerParams(vmem_limit_bytes=(64 if manual else limit) * 2**20),
        cost_estimate=pl.CostEstimate(flops=flops, bytes_accessed=nbytes, transcendentals=0),
    )(*arrays)


def shape(*dims, dtype=BF):
    return jax.ShapeDtypeStruct(dims, dtype)


def key_scratch(rows):
    return [pltpu.VMEM((rows, D), BF), pltpu.VMEM((D, rows), BF), pltpu.VMEM((16, rows), BF)]


def local_part(level, x, fill, gains, qw, kw, vw, rows, manual):
    return call(
        functools.partial(local_kernel, level, rows),
        [shape(HEADS, rows, 128), shape(HEADS, VROWS, rows, dtype=F32),
         shape(16, 128, dtype=F32), shape(16, 128, dtype=F32)],
        [x, fill, gains, (qw, level), (kw, level), (vw, level)],
        scratch=key_scratch(rows),
        flops=8 * rows * rows * 512 * 2,
        manual=manual,
    )


def finish_part(kernel, args, raw, outs, rows, count, manual, extra=(), away=()):
    return call(
        kernel,
        outs,
        args,
        raw=set(range(raw)),
        scratch=[
            pltpu.VMEM((D, rows), BF),
            *key_scratch(count),
            pltpu.VMEM((rows, D), BF),
            pltpu.VMEM((2 * rows, D), BF),
            pltpu.VMEM((D, 2 * rows), BF),
            *extra,
        ],
        flops=8 * rows * count * 512 * 2 + 4 * rows * D * D,
        manual=manual,
        away=away,
    )


def per_device(points, tree_order, present, gain_attn, query_weight, key_weight, value_weight,
               out_weight, gain_mlp, hidden_weight, proj_weight):
    size = lax.axis_size("leaf")

    def trade(value, bit):
        return lax.ppermute(value, "leaf", [(s, s ^ (1 << bit)) for s in range(size)])

    base = size.bit_length() - 1 - 3
    fill0 = present.reshape(1, 1024)
    parts = []
    for first, last in ((0, 1), (1, len(SENT))):
        parts += call(
            functools.partial(front_kernel, first),
            [shape(count + (0 if first else 16), D) for count in SENT[first:last]],
            [points, fill0], flops=10**9, manual=True)
    chunks = [trade(part, base) for part in parts[:-1]]
    tree4 = tree_order.reshape(256, 4)
    tree_rows = tree4.T

    def kvs(level):
        return [(key_weight, level), (value_weight, level)]

    q, o, qp, kp = local_part(0, points, fill0, gain_attn, query_weight, key_weight,
                              value_weight, 1024, True)
    line, lane = SENT[0] + USUAL // D, USUAL % D
    over = jnp.maximum(parts[0][line, lane], chunks[0][line, lane]) > 0
    over, left, q, tree_rows = lax.optimization_barrier((over, parts[-1], q, tree_rows))
    rest = lax.cond(over, lambda left: trade(left, base), lambda left: left, left)
    rest, o = lax.optimization_barrier((rest, o))
    o, kp = call(
        remote_kernel, [shape(HEADS, VROWS, 1024, dtype=F32), shape(16, 128, dtype=F32)],
        [chunks[0], gain_attn, *kvs(0), q, o, kp],
        scratch=key_scratch(EARLY),
        flops=10**10, manual=True)
    chunks.append(rest)
    y0, x1 = finish_part(
        finish0_kernel,
        [*chunks, *chunks[:3], fill0, gain_attn, *kvs(0), q, o, qp, kp, (out_weight, 0), points,
         tree4, chunks[3]],
        len(SENT), [shape(1024, D), shape(528, D)], 1024, USUAL - EARLY, True,
        extra=[*key_scratch(SENT[-1]), pltpu.VMEM((16, 128), F32)])
    far1 = trade(x1, base + 1)
    q, o, qp, kp = local_part(1, x1, fill0, gain_attn, query_weight, key_weight, value_weight,
                              512, False)
    y1, x2 = finish_part(
        finish1_kernel,
        [far1, far1, gain_attn, *kvs(1), q, o, qp, kp, x1, (out_weight, 1)],
        1, [shape(512, D), shape(272, D)], 512, 512, False, away={0, 1})
    far2 = trade(x2, base + 2)
    q, o, qp, kp = local_part(2, x2, fill0, gain_attn, query_weight, key_weight, value_weight,
                              256, True)
    (field,) = finish_part(
        finish2_kernel,
        [far2, far2, gain_attn, *kvs(2), q, o, qp, kp, x2, (out_weight, 2),
         gain_mlp.reshape(1, D), (hidden_weight, None), (proj_weight, None), y1, y0, tree_rows],
        1, [shape(1024, D)], 256, 256, True)
    return field


def solution(mesh):
    placed = (
        P(("cloud", "leaf"), None),
        P(("cloud", "leaf")),
        P(("cloud", "leaf")),
        P(), P(), P(), P(), P(), P(), P(), P(),
    )
    return jax.shard_map(
        per_device,
        mesh=mesh,
        in_specs=placed,
        out_specs=P(("cloud", "leaf"), None),
        check_vma=False,
    )
```

```python
import functools
import jax
import jax.numpy as jnp
from jax import lax
from jax.experimental import pallas as pl
from jax.experimental.pallas import tpu as pltpu
from jax.sharding import PartitionSpec as P

D = 512
HEAD = 64
HEADS = 8
VROWS = 80
LIMIT2 = 60.0**2
QSCALE = HEAD ** (-0.5)
NT = (((1,), (1,)), ((), ()))
TN = (((0,), (0,)), ((), ()))
BF = jnp.bfloat16
F32 = jnp.float32
ANY = pl.BlockSpec(memory_space=pl.ANY)
VMEM = pl.BlockSpec(memory_space=pltpu.VMEM)
FLAT = 1024 * 576
SENT = (384, 224, 224, 192)
USUAL = sum(SENT[:-1])
EARLY = SENT[0]


def dotf(a, b, dims=(((1,), (0,)), ((), ()))):
    return lax.dot_general(a, b, dims, preferred_element_type=F32)


def norm_rows(values, gain):
    wide = values.astype(F32)
    centre = jnp.mean(wide, axis=-1, keepdims=True)
    wide = wide - centre
    spread = jnp.mean(jnp.square(wide), axis=-1, keepdims=True)
    return (wide * lax.rsqrt(spread + 1e-05) * gain).astype(BF)


def to_column(row):
    eye = lax.broadcasted_iota(jnp.int32, (128, 128), 0) == lax.broadcasted_iota(
        jnp.int32, (128, 128), 1
    )
    parts = []
    for start in range(0, row.shape[1], 128):
        block = jnp.where(eye, row[:, start : start + 128], 0.0)
        parts.append(jnp.sum(block, axis=1, keepdims=True))
    return jnp.concatenate(parts, axis=0)


def head_select():
    lane = lax.broadcasted_iota(jnp.int32, (16, D), 1)
    head = lax.broadcasted_iota(jnp.int32, (16, D), 0)
    return jnp.where(lane // HEAD == head, 1.0, 0.0).astype(BF)


def head_peak(rows):
    wide = rows.astype(F32)
    sums = dotf(head_select(), (wide * wide).astype(BF), NT)
    return jnp.broadcast_to(jnp.max(sums, axis=1, keepdims=True), (16, 128))


def split_queries(queries, q_ref):
    low = lax.broadcasted_iota(jnp.int32, (1, 128), 1) < HEAD
    for pair in range(HEADS // 2):
        part = queries[:, pair * 128 : (pair + 1) * 128]
        q_ref[2 * pair] = jnp.where(low, part, jnp.zeros_like(part))
        q_ref[2 * pair + 1] = jnp.where(low, jnp.zeros_like(part), part)


def fill_rows(fill_row):
    first = lax.broadcasted_iota(jnp.int32, (16, fill_row.shape[1]), 0) == 0
    return jnp.where(first, fill_row, 0.0).astype(BF)


def attend(q_ref, k_ref, vt_ref, ones_ref, o_ref, add_ref):
    count = k_ref.shape[0]
    blocks = [(start, min(256, count - start)) for start in range(0, count, 256)]
    depth = 2 if q_ref.shape[1] > 256 else 3

    def run(pairs, columns):
        waiting, totals = [], {}

        def drain():
            pair, head, block, scores = waiting.pop(0)
            start, size = block
            weights = jnp.exp(scores).astype(BF)
            keys = slice(start, start + size)
            values = vt_ref[columns(2 * pair + head, HEAD), keys]
            part = dotf(jnp.concatenate([values, ones_ref[:, keys]], axis=0), weights)
            total = totals.pop(head, None)
            total = part if total is None else total + part
            if block == blocks[-1]:
                if add_ref is not None:
                    total = total + add_ref[pair * 2 + head]
                o_ref[pair * 2 + head] = total
            else:
                totals[head] = total

        for pair in pairs:
            for head in range(2):
                queries = q_ref[2 * pair + head]
                for block in blocks:
                    start, size = block
                    keys = k_ref[start : start + size, columns(pair, 128)]
                    waiting.append((pair, head, block, dotf(keys, queries, NT)))
                    if len(waiting) > depth:
                        drain()
        while waiting:
            drain()

    if q_ref.shape[1] * count <= FLAT:
        run(range(HEADS // 2), lambda at, size: slice(at * size, (at + 1) * size))
        return

    def body(pair, carry):
        run([pair], lambda at, size: pl.ds(pl.multiple_of(at * size, size), size))
        return carry

    lax.fori_loop(0, HEADS // 2, body, 0)


def project_kv(normed, kw, vw, fill_row=None):
    keys = dotf(normed, kw.here[...]).astype(BF)
    values_t = dotf(vw.here[...], normed, (((0,), (1,)), ((), ())))
    if fill_row is not None:
        values_t = values_t * fill_row
    return keys, values_t.astype(BF)


def front_kernel(first, points, present, *outs):
    fill = present.here[...].astype(F32)
    upto = lax.broadcasted_iota(jnp.int32, (1024, 1024), 0) <= lax.broadcasted_iota(
        jnp.int32, (1024, 1024), 1
    )
    f8 = jnp.broadcast_to(fill, (8, 1024)).astype(BF)
    rank = dotf(f8, jnp.where(upto, 1.0, 0.0).astype(BF))[:1]
    place = jnp.where(fill > 0.0, rank - 1.0, -1.0).astype(jnp.int32)
    at = sum(SENT[:first])
    for out, count in zip(outs, SENT[first:]):
        rows = lax.broadcasted_iota(jnp.int32, (count, 1024), 0) + at
        pick = jnp.where(rows == place, 1.0, 0.0).astype(BF)
        out.ref[:count, :] = dotf(pick, points.here[...]).astype(BF)
        if at == 0:
            lane = lax.broadcasted_iota(jnp.int32, (16, D), 1)
            line = lax.broadcasted_iota(jnp.int32, (16, D), 0)
            total = jnp.broadcast_to(rank[:, 1023:], (16, D)).astype(jnp.int32)
            out.ref[count:, :] = jnp.where(line * D + lane < total, 1.0, 0.0).astype(BF)
        out.flush()
        at += count


def pooled_places(order_row):
    lanes = lax.broadcasted_iota(jnp.int32, (1024, 1024), 1).astype(F32)
    chosen = jnp.where(to_column(order_row) == lanes, 1.0, 0.0).astype(BF)
    row = lax.broadcasted_iota(jnp.int32, (8, 1024), 1)
    line = lax.broadcasted_iota(jnp.int32, (8, 1024), 0)
    both = dotf(jnp.where(line == 0, row // 4, (row // 2) % 2).astype(F32).astype(BF), chosen)
    return both[:1] + 256.0 * both[1:2]


def local_kernel(level, rows, x, fill_src, gains, qw, kw, vw, *refs):
    if level == 0:
        order, q, o, qp, kp, spot, k_ref, vt_ref, ones_ref = refs
        spot.ref[...] = jnp.broadcast_to(pooled_places(order.here[...].astype(F32)), (8, 1024))
        spot.flush()
    else:
        q, o, qp, kp, k_ref, vt_ref, ones_ref = refs
    normed = norm_rows(x.here[:rows, :], gains.here[level : level + 1, :])
    if level == 0:
        fill = fill_src.here[...].astype(F32)
        normed = normed * to_column(fill).astype(BF)
    else:
        fill = x.here[rows : rows + 1, :rows].astype(F32)
    queries = dotf(normed, qw.here[...]).astype(BF) * QSCALE
    split_queries(queries, q.ref)
    q.flush()
    keys, values_t = project_kv(normed, kw, vw)
    qp.ref[...] = head_peak(queries)
    kp.ref[...] = head_peak(keys)
    qp.flush()
    kp.flush()
    k_ref[...] = keys
    vt_ref[...] = (values_t.astype(F32) * fill).astype(BF)
    ones_ref[...] = fill_rows(fill)
    attend(q.ref, k_ref, vt_ref, ones_ref, o.ref, None)
    if level == 0:
        for head in range(HEADS):
            o.ref[head, HEAD : HEAD + 1, :] += 1.0 - fill
    else:
        prod = queries.astype(F32) * keys.astype(F32)
        high = prod.astype(BF)
        rest = (prod - high.astype(F32)).astype(BF)
        select = head_select()
        own = jnp.exp(dotf(select, high, NT) + dotf(select, rest, NT))
        own = own * (1.0 - fill)
        for head in range(HEADS):
            weight = own[head : head + 1]
            part = values_t[head * HEAD : (head + 1) * HEAD].astype(F32)
            o.ref[head, :HEAD, :] += part * weight
            o.ref[head, HEAD : HEAD + 1, :] += weight
    o.flush()


def far_fill(packed):
    at = packed.shape[0] - 16
    return jnp.concatenate([packed[at : at + 1, :], packed[at + 1 : at + 2, :]], axis=1).astype(F32)


def remote_kernel(first, gains, kw, vw, q, o_in, kp_in, mine, o, kp, over, k_ref, vt_ref,
                  ones_ref):
    normed = norm_rows(first.here[:EARLY, :], gains.here[0:1, :])
    fill = far_fill(first.here)[:, :EARLY]
    keys, values_t = project_kv(normed, kw, vw, fill)
    k_ref[...] = keys
    vt_ref[...] = values_t
    ones_ref[...] = fill_rows(fill)
    kp.ref[...] = jnp.maximum(kp_in.here[...], head_peak(keys))
    kp.flush()
    used = far_fill(first.here) + far_fill(mine.here)
    over.ref[...] = jnp.broadcast_to(used[:, USUAL : USUAL + 1], (8, 128)).astype(jnp.int32)
    over.flush()
    attend(q.here, k_ref, vt_ref, ones_ref, o.ref, o_in.here)
    o.flush()


def exact_attend(level, q_ref, own, fills, chunks, counts, gains, kw, vw, att_ref, xbuf, kf, vf):
    rows = q_ref.shape[1]
    for side, sources in enumerate(([(own, rows)], list(zip(chunks, counts)))):
        at = 0
        for ref, count in sources:
            pltpu.sync_copy(ref.at[pl.ds(0, count), :], xbuf.at[pl.ds(at, count), :])
            at += count
        for start in range(0, rows, 128):
            normed = norm_rows(xbuf[start : start + 128, :], gains.here[level : level + 1, :])
            if level == 0 and side == 0:
                normed = normed * to_column(fills[0][:, start : start + 128]).astype(BF)
            keys, values_t = project_kv(normed, kw, vw)
            base = side * rows + start
            kf[base : base + 128, :] = keys
            vf[:, base : base + 128] = values_t
    total = 2 * rows
    fill8 = jnp.broadcast_to(jnp.concatenate(fills, axis=1), (8, total)).astype(BF)
    width = 128

    def body(step, carry):
        pair = step // (rows // width)
        start = pl.multiple_of(step % (rows // width) * width, width)
        lanes = pl.ds(pl.multiple_of(pair * 128, 128), 128)
        keys = kf[:, lanes]
        mask = dotf(fill8, jnp.ones((8, width), BF), TN) > 0.5
        own = lax.broadcasted_iota(jnp.int32, (total, width), 0) == (
            lax.broadcasted_iota(jnp.int32, (total, width), 1) + start
        )
        allowed = mask | own
        for head in range(2):
            queries = q_ref[2 * pair + head, pl.ds(start, width), :]
            scores = jnp.where(allowed, dotf(keys, queries, NT), -1e30)
            weights = jnp.exp(scores - jnp.max(scores, axis=0, keepdims=True))
            weights = weights / jnp.sum(weights, axis=0, keepdims=True)
            first = pl.multiple_of(pair * 128 + head * HEAD, HEAD)
            values = vf[pl.ds(first, HEAD), :]
            att_ref[pl.ds(first, HEAD), pl.ds(start, width)] = dotf(
                values, weights.astype(BF)
            ).astype(BF)
        return carry

    lax.fori_loop(0, HEADS // 2 * (rows // width), body, 0)


def finish_attention(level, far, chunk_refs, counts, operands, scratch, fill, fill_far, rest=None):
    gains, kw, vw, q, qp, kp, o, own = operands
    att_ref, k_ref, vt_ref, ones_ref, xbuf, kf, vf = scratch[:7]
    gain = gains.here[level : level + 1, :]
    begin = 0 if rest is None else EARLY
    usual = begin + k_ref.shape[0]
    normed = [norm_rows(x.here[:count, :], gain) for x, count in zip(far, counts)]
    normed = jnp.concatenate(normed, axis=0) if len(normed) > 1 else normed[0]
    keys, values_t = project_kv(normed, kw, vw, fill_far[:, begin:usual])
    k_ref[...] = keys
    vt_ref[...] = values_t
    ones_ref[...] = fill_rows(fill_far[:, begin:usual])
    attend(q.here, k_ref, vt_ref, ones_ref, o.here, o.here)
    peak = jnp.maximum(kp.here[...], head_peak(keys)) * qp.here[...]
    own.here
    if rest is not None:
        rest_k, rest_vt, rest_ones, rest_peak = scratch[7:]
        rest_peak[...] = jnp.zeros_like(rest_peak)
        rest.here

        @pl.when(jnp.max(fill_far[:, usual:]) > 0.0)
        def _():
            keys, values_t = project_kv(
                norm_rows(rest.here[...], gain), kw, vw, fill_far[:, usual:])
            rest_k[...] = keys
            rest_vt[...] = values_t
            rest_ones[...] = fill_rows(fill_far[:, usual:])
            rest_peak[...] = head_peak(keys)
            attend(q.here, rest_k, rest_vt, rest_ones, o.here, o.here)

        peak = jnp.maximum(peak, rest_peak[...] * qp.here[...])
    for head in range(HEADS):
        scale = 1.0 / o.here[head, HEAD : HEAD + 1, :]
        att_ref[head * HEAD : (head + 1) * HEAD, :] = (o.here[head, :HEAD, :] * scale).astype(BF)
    inside = jnp.max(peak) <= LIMIT2

    @pl.when(jnp.logical_not(inside))
    def _():
        exact_attend(level, q.here, own.here, [fill, fill_far], chunk_refs,
                     counts if rest is None else SENT, gains, kw, vw, att_ref, xbuf, kf, vf)

    return att_ref[...]


def finish0_kernel(*refs):
    chunks = refs[: len(SENT)]
    (packed, second, third, fill_ref, gains, kw, vw, q, o, qp, kp, ow, points, tree, rest,
     y_out, x1_out) = refs[len(SENT) : len(SENT) + 17]
    scratch = refs[len(SENT) + 17 :]
    fill = fill_ref.here[...].astype(F32)
    attended_t = finish_attention(
        0, [second, third], chunks, SENT[1:3], (gains, kw, vw, q, qp, kp, o, points), scratch,
        fill, far_fill(packed.here), rest)
    x0 = points.here[...].astype(F32) * to_column(fill)
    y = (x0 + dotf(attended_t, ow.here[...], TN)).astype(BF)
    y_out.ref[...] = y
    y_out.flush()
    f8 = jnp.broadcast_to(fill, (8, 1024)).astype(BF)
    place = tree.here[:1, :]
    fills = []
    for half in range(2):
        rows = (lax.broadcasted_iota(jnp.int32, (256, 1024), 0) + 256 * half).astype(F32)
        pool = jnp.where(rows == place, 0.5, 0.0).astype(BF)
        x1_out.ref[half * 256 : (half + 1) * 256, :] = dotf(pool, y).astype(BF)
        fills.append(jnp.where(dotf(f8, pool, NT)[:1] > 0.25, 1.0, 0.0))
    x1_out.ref[512:, :] = jnp.broadcast_to(jnp.concatenate(fills, axis=1), (16, D)).astype(BF)
    x1_out.flush()


def finish1_kernel(far_hbm, last, gains, kw, vw, q, o_in, qp, kp, x, ow, y_out, x2_out, *scratch):
    fill = x.here[512:513, :].astype(F32)
    attended_t = finish_attention(
        1, [last], [far_hbm], (512,), (gains, kw, vw, q, qp, kp, o_in, x), scratch, fill,
        last.here[512:513, :].astype(F32))
    y = (x.here[:512, :].astype(F32) + dotf(attended_t, ow.here[...], TN)).astype(BF)
    wide = y.astype(F32)
    x2_out.ref[:256, :] = ((wide[:256] + wide[256:]) * 0.5).astype(BF)
    f_next = jnp.maximum(fill[:, :256], fill[:, 256:])
    x2_out.ref[256:, :] = jnp.broadcast_to(
        jnp.concatenate([f_next, f_next], axis=1), (16, D)).astype(BF)
    x2_out.flush()
    y_out.ref[...] = y
    y_out.flush()


def finish2_kernel(far_hbm, last, gains, kw, vw, q, o_in, qp, kp, x, ow, gm, hw, pw, y1, y0, tree,
                   field, *scratch):
    fill = x.here[256:257, :256].astype(F32)
    attended_t = finish_attention(
        2, [last], [far_hbm], (256,), (gains, kw, vw, q, qp, kp, o_in, x), scratch, fill,
        last.here[256:257, :256].astype(F32))
    y2 = (x.here[:256, :].astype(F32) + dotf(attended_t, ow.here[...], TN)).astype(BF)
    normed = norm_rows(y2, gm.here[...])
    hw.here, pw.here
    total = y2.astype(F32)
    before = None
    for start in range(0, 2048 + 512, 512):
        if start < 2048:
            now = dotf(normed, hw.here[:, start : start + 512])
        if before is not None:
            hidden = jax.nn.gelu(before, approximate=True).astype(BF)
            total = total + dotf(hidden, pw.here[start - 512 : start, :])
        before = now
    top = total.astype(BF).astype(F32)
    up = [(y1.here[half * 256 : (half + 1) * 256, :].astype(F32) + top).astype(BF)
          for half in range(2)]
    place = to_column(tree.here[:1, :])
    lanes = lax.broadcasted_iota(jnp.int32, (256, 256), 1).astype(F32)
    for side, out in enumerate(field.parts(4)):
        total = y0.here[256 * side : 256 * (side + 1), :].astype(F32)
        for half in range(2):
            picked = place[256 * side : 256 * (side + 1)] == lanes + 256.0 * half
            total = total + dotf(jnp.where(picked, 1.0, 0.0).astype(BF), up[half])
        field.ref[256 * side : 256 * (side + 1), :] = total.astype(BF)
        out.start()


class Here:
    def __init__(self, ref, copy=None):
        self.here = self.ref = ref
        self.copy = copy

    def flush(self):
        if self.copy is not None:
            self.copy.start()

    def parts(self, count):
        rows = self.ref.shape[0] // count
        source, target, sem = self.ends
        return [
            pltpu.make_async_copy(
                source.at[pl.ds(i * rows, rows), :], target.at[pl.ds(i * rows, rows), :], sem)
            for i in range(count)
        ]


class Piece:
    def __init__(self, copy, ref):
        self.copy, self.ref = copy, ref

    @property
    def here(self):
        if self.copy is not None:
            self.copy.wait()
            self.copy = None
        return self.ref


def call(kernel, outs, args, raw=(), scratch=(), flops=0, limit=64, manual=False, away=()):
    arrays = [a[0] if isinstance(a, tuple) else a for a in args]
    n, m = len(args), len(outs)
    moved = [i for i in range(n) if isinstance(args[i], tuple) or (manual and i not in raw)]
    level = [args[i][1] if isinstance(args[i], tuple) else None for i in range(n)]
    buffers = [
        pltpu.VMEM(arrays[i].shape if level[i] is None else arrays[i].shape[1:], arrays[i].dtype)
        for i in moved
    ]
    away = list(range(m)) if manual else sorted(away)
    sems = [pltpu.SemaphoreType.DMA((len(moved),))] if moved else []
    if away:
        buffers = [pltpu.VMEM(outs[i].shape, outs[i].dtype) for i in away] + buffers
        sems.append(pltpu.SemaphoreType.DMA((m,)))

    def body(*refs):
        sources, targets, rest = refs[:n], refs[n : n + m], list(refs[n + m :])
        results = [Here(t) for t in targets]
        held, rest = rest[: len(away)], rest[len(away) :]
        slots, rest = rest[: len(moved)], rest[len(moved) :]
        operands = [s if i in raw else Here(s) for i, s in enumerate(sources)]
        if moved:
            sem = rest.pop(0)
        if away:
            out_sem = rest.pop(0)
        for i, h in zip(away, held):
            results[i] = Here(h, pltpu.make_async_copy(h, targets[i], out_sem.at[i]))
            results[i].ends = (h, targets[i], out_sem.at[i])
        for slot, i in enumerate(moved):
            source = sources[i] if level[i] is None else sources[i].at[level[i]]
            copy = pltpu.make_async_copy(source, slots[slot], sem.at[slot])
            copy.start()
            operands[i] = Piece(copy, slots[slot])
        kernel(*operands, *results, *rest)
        for i in moved:
            operands[i].here
        for i in away:
            results[i].copy.wait()

    nbytes = sum(a.size * a.dtype.itemsize for a in arrays) + sum(
        a.size * a.dtype.itemsize for a in outs)
    return pl.pallas_call(
        body,
        out_shape=outs,
        in_specs=[ANY if manual or i in raw or i in moved else VMEM for i in range(n)],
        out_specs=[ANY if i in away else VMEM for i in range(m)],
        scratch_shapes=buffers + sems + list(scratch),
        compiler_params=pltpu.CompilerParams(vmem_limit_bytes=limit * 2**20),
        cost_estimate=pl.CostEstimate(flops=flops, bytes_accessed=nbytes, transcendentals=0),
    )(*arrays)


def shape(*dims, dtype=BF):
    return jax.ShapeDtypeStruct(dims, dtype)


def key_scratch(rows):
    return [pltpu.VMEM((rows, D), BF), pltpu.VMEM((D, rows), BF), pltpu.VMEM((16, rows), BF)]


def local_part(level, x, fill, gains, qw, kw, vw, rows, manual, order=()):
    return call(
        functools.partial(local_kernel, level, rows),
        [shape(HEADS, rows, 128), shape(HEADS, VROWS, rows, dtype=F32),
         shape(16, 128, dtype=F32), shape(16, 128, dtype=F32)]
        + [shape(8, rows, dtype=F32) for _ in order],
        [x, fill, gains, (qw, level), (kw, level), (vw, level), *order],
        scratch=key_scratch(rows),
        flops=8 * rows * rows * 512 * 2,
        manual=manual,
        limit={0: 64, 1: 16, 2: 12}[level],
    )


def finish_part(kernel, args, raw, outs, rows, count, manual, extra=(), away=()):
    return call(
        kernel,
        outs,
        args,
        raw=set(range(raw)),
        scratch=[
            pltpu.VMEM((D, rows), BF),
            *key_scratch(count),
            pltpu.VMEM((rows, D), BF),
            pltpu.VMEM((2 * rows, D), BF),
            pltpu.VMEM((D, 2 * rows), BF),
            *extra,
        ],
        flops=8 * rows * count * 512 * 2 + 4 * rows * D * D,
        manual=manual,
        away=away,
        limit={1024: 64, 512: 16, 256: 24}[rows],
    )


def per_device(points, tree_order, present, gain_attn, query_weight, key_weight, value_weight,
               out_weight, gain_mlp, hidden_weight, proj_weight):
    size = lax.axis_size("leaf")

    def trade(value, bit):
        return lax.ppermute(value, "leaf", [(s, s ^ (1 << bit)) for s in range(size)])

    base = size.bit_length() - 1 - 3
    fill0 = present.reshape(1, 1024)
    parts = []
    for first, last in ((0, 1), (1, len(SENT))):
        parts += call(
            functools.partial(front_kernel, first),
            [shape(count + (0 if first else 16), D) for count in SENT[first:last]],
            [points, fill0], flops=10**9, manual=True)
    chunks = [trade(part, base) for part in parts[:-1]]

    def kvs(level):
        return [(key_weight, level), (value_weight, level)]

    q, o, qp, kp, spot = local_part(0, points, fill0, gain_attn, query_weight, key_weight,
                                    value_weight, 1024, True, [tree_order.reshape(1, 1024)])
    o, kp, over = call(
        remote_kernel,
        [shape(HEADS, VROWS, 1024, dtype=F32), shape(16, 128, dtype=F32),
         shape(8, 128, dtype=jnp.int32)],
        [chunks[0], gain_attn, *kvs(0), q, o, kp, parts[0]],
        scratch=key_scratch(EARLY), flops=10**10, manual=True)
    chunks.append(lax.cond(
        over[0, 0] > 0, lambda left: trade(left, base), lambda left: left, parts[-1]))
    y0, x1 = finish_part(
        finish0_kernel,
        [*chunks, *chunks[:3], fill0, gain_attn, *kvs(0), q, o, qp, kp, (out_weight, 0), points,
         spot, chunks[3]],
        len(SENT), [shape(1024, D), shape(528, D)], 1024, USUAL - EARLY, True,
        extra=[*key_scratch(SENT[-1]), pltpu.VMEM((16, 128), F32)])
    far1 = trade(x1, base + 1)
    q, o, qp, kp = local_part(1, x1, fill0, gain_attn, query_weight, key_weight, value_weight,
                              512, False)
    y1, x2 = finish_part(
        finish1_kernel,
        [far1, far1, gain_attn, *kvs(1), q, o, qp, kp, x1, (out_weight, 1)],
        1, [shape(512, D), shape(272, D)], 512, 512, False, away={0, 1})
    far2 = trade(x2, base + 2)
    q, o, qp, kp = local_part(2, x2, fill0, gain_attn, query_weight, key_weight, value_weight,
                              256, True)
    (field,) = finish_part(
        finish2_kernel,
        [far2, far2, gain_attn, *kvs(2), q, o, qp, kp, x2, (out_weight, 2),
         gain_mlp.reshape(1, D), (hidden_weight, None), (proj_weight, None), y1, y0, spot],
        1, [shape(1024, D)], 256, 256, True)
    return field


def solution(mesh):
    placed = (
        P(("cloud", "leaf"), None),
        P(("cloud", "leaf")),
        P(("cloud", "leaf")),
        P(), P(), P(), P(), P(), P(), P(), P(),
    )
    return jax.shard_map(
        per_device,
        mesh=mesh,
        in_specs=placed,
        out_specs=P(("cloud", "leaf"), None),
        check_vma=False,
    )
```

```python
import functools
import jax
import jax.numpy as jnp
from jax import lax
from jax.experimental import pallas as pl
from jax.experimental.pallas import tpu as pltpu
from jax.sharding import PartitionSpec as P

D = 512
HEAD = 64
HEADS = 8
VROWS = 80
LIMIT2 = 60.0**2
QSCALE = HEAD ** (-0.5)
NT = (((1,), (1,)), ((), ()))
TN = (((0,), (0,)), ((), ()))
BF = jnp.bfloat16
F32 = jnp.float32
ANY = pl.BlockSpec(memory_space=pl.ANY)
VMEM = pl.BlockSpec(memory_space=pltpu.VMEM)
FLAT = 1024 * 576
SENT = (352, 240, 240, 192)
USUAL = sum(SENT[:-1])
EARLY = SENT[0]


def dotf(a, b, dims=(((1,), (0,)), ((), ()))):
    return lax.dot_general(a, b, dims, preferred_element_type=F32)


def norm_rows(values, gain):
    wide = values.astype(F32)
    centre = jnp.mean(wide, axis=-1, keepdims=True)
    wide = wide - centre
    spread = jnp.mean(jnp.square(wide), axis=-1, keepdims=True)
    return (wide * lax.rsqrt(spread + 1e-05) * gain).astype(BF)


def to_column(row):
    eye = lax.broadcasted_iota(jnp.int32, (128, 128), 0) == lax.broadcasted_iota(
        jnp.int32, (128, 128), 1
    )
    parts = []
    for start in range(0, row.shape[1], 128):
        block = jnp.where(eye, row[:, start : start + 128], 0.0)
        parts.append(jnp.sum(block, axis=1, keepdims=True))
    return jnp.concatenate(parts, axis=0)


def head_select():
    lane = lax.broadcasted_iota(jnp.int32, (16, D), 1)
    head = lax.broadcasted_iota(jnp.int32, (16, D), 0)
    return jnp.where(lane // HEAD == head, 1.0, 0.0).astype(BF)


def head_peak(rows):
    wide = rows.astype(F32)
    sums = dotf(head_select(), (wide * wide).astype(BF), NT)
    return jnp.broadcast_to(jnp.max(sums, axis=1, keepdims=True), (16, 128))


def split_queries(queries, q_ref):
    low = lax.broadcasted_iota(jnp.int32, (1, 128), 1) < HEAD
    for pair in range(HEADS // 2):
        part = queries[:, pair * 128 : (pair + 1) * 128]
        q_ref[2 * pair] = jnp.where(low, part, jnp.zeros_like(part))
        q_ref[2 * pair + 1] = jnp.where(low, jnp.zeros_like(part), part)


def fill_rows(fill_row):
    first = lax.broadcasted_iota(jnp.int32, (16, fill_row.shape[1]), 0) == 0
    return jnp.where(first, fill_row, 0.0).astype(BF)


def attend(q_ref, k_ref, vt_ref, ones_ref, o_ref, add_ref):
    count = k_ref.shape[0]
    blocks = [(start, min(256, count - start)) for start in range(0, count, 256)]
    depth = 2 if q_ref.shape[1] > 256 else 3

    def run(pairs, columns):
        waiting, totals = [], {}

        def drain():
            pair, head, block, scores = waiting.pop(0)
            start, size = block
            weights = jnp.exp(scores).astype(BF)
            keys = slice(start, start + size)
            values = vt_ref[columns(2 * pair + head, HEAD), keys]
            part = dotf(jnp.concatenate([values, ones_ref[:, keys]], axis=0), weights)
            total = totals.pop(head, None)
            total = part if total is None else total + part
            if block == blocks[-1]:
                if add_ref is not None:
                    total = total + add_ref[pair * 2 + head]
                o_ref[pair * 2 + head] = total
            else:
                totals[head] = total

        for pair in pairs:
            for head in range(2):
                queries = q_ref[2 * pair + head]
                for block in blocks:
                    start, size = block
                    keys = k_ref[start : start + size, columns(pair, 128)]
                    waiting.append((pair, head, block, dotf(keys, queries, NT)))
                    if len(waiting) > depth:
                        drain()
        while waiting:
            drain()

    if q_ref.shape[1] * count <= FLAT:
        run(range(HEADS // 2), lambda at, size: slice(at * size, (at + 1) * size))
        return

    def body(pair, carry):
        run([pair], lambda at, size: pl.ds(pl.multiple_of(at * size, size), size))
        return carry

    lax.fori_loop(0, HEADS // 2, body, 0)


def project_kv(normed, kw, vw, fill_row=None):
    keys = dotf(normed, kw.here[...]).astype(BF)
    values_t = dotf(vw.here[...], normed, (((0,), (1,)), ((), ())))
    if fill_row is not None:
        values_t = values_t * fill_row
    return keys, values_t.astype(BF)


def front_kernel(first, points, present, *outs):
    fill = present.here[...].astype(F32)
    upto = lax.broadcasted_iota(jnp.int32, (1024, 1024), 0) <= lax.broadcasted_iota(
        jnp.int32, (1024, 1024), 1
    )
    f8 = jnp.broadcast_to(fill, (8, 1024)).astype(BF)
    rank = dotf(f8, jnp.where(upto, 1.0, 0.0).astype(BF))[:1]
    place = jnp.where(fill > 0.0, rank - 1.0, -1.0).astype(jnp.int32)
    at = sum(SENT[:first])
    for out, count in zip(outs, SENT[first:]):
        rows = lax.broadcasted_iota(jnp.int32, (count, 1024), 0) + at
        pick = jnp.where(rows == place, 1.0, 0.0).astype(BF)
        out.ref[:count, :] = dotf(pick, points.here[...]).astype(BF)
        if at == 0:
            lane = lax.broadcasted_iota(jnp.int32, (16, D), 1)
            line = lax.broadcasted_iota(jnp.int32, (16, D), 0)
            total = jnp.broadcast_to(rank[:, 1023:], (16, D)).astype(jnp.int32)
            out.ref[count:, :] = jnp.where(line * D + lane < total, 1.0, 0.0).astype(BF)
        out.flush()
        at += count


def pooled_places(order_row):
    lanes = lax.broadcasted_iota(jnp.int32, (1024, 1024), 1).astype(F32)
    chosen = jnp.where(to_column(order_row) == lanes, 1.0, 0.0).astype(BF)
    row = lax.broadcasted_iota(jnp.int32, (8, 1024), 1)
    line = lax.broadcasted_iota(jnp.int32, (8, 1024), 0)
    both = dotf(jnp.where(line == 0, row // 4, (row // 2) % 2).astype(F32).astype(BF), chosen)
    return both[:1] + 256.0 * both[1:2]


def local_kernel(level, rows, x, fill_src, gains, qw, kw, vw, *refs):
    if level == 0:
        order, q, o, qp, kp, spot, k_ref, vt_ref, ones_ref = refs
        spot.ref[...] = jnp.broadcast_to(pooled_places(order.here[...].astype(F32)), (8, 1024))
        spot.flush()
    else:
        q, o, qp, kp, k_ref, vt_ref, ones_ref = refs
    normed = norm_rows(x.here[:rows, :], gains.here[level : level + 1, :])
    if level == 0:
        fill = fill_src.here[...].astype(F32)
        normed = normed * to_column(fill).astype(BF)
    else:
        fill = x.here[rows : rows + 1, :rows].astype(F32)
    queries = dotf(normed, qw.here[...]).astype(BF) * QSCALE
    split_queries(queries, q.ref)
    q.flush()
    keys, values_t = project_kv(normed, kw, vw)
    qp.ref[...] = head_peak(queries)
    kp.ref[...] = head_peak(keys)
    qp.flush()
    kp.flush()
    k_ref[...] = keys
    vt_ref[...] = (values_t.astype(F32) * fill).astype(BF)
    ones_ref[...] = fill_rows(fill)
    attend(q.ref, k_ref, vt_ref, ones_ref, o.ref, None)
    if level == 0:
        for head in range(HEADS):
            o.ref[head, HEAD : HEAD + 1, :] += 1.0 - fill
    else:
        prod = queries.astype(F32) * keys.astype(F32)
        high = prod.astype(BF)
        rest = (prod - high.astype(F32)).astype(BF)
        select = head_select()
        own = jnp.exp(dotf(select, high, NT) + dotf(select, rest, NT))
        own = own * (1.0 - fill)
        for head in range(HEADS):
            weight = own[head : head + 1]
            part = values_t[head * HEAD : (head + 1) * HEAD].astype(F32)
            o.ref[head, :HEAD, :] += part * weight
            o.ref[head, HEAD : HEAD + 1, :] += weight
    o.flush()


def far_fill(packed):
    at = packed.shape[0] - 16
    return jnp.concatenate([packed[at : at + 1, :], packed[at + 1 : at + 2, :]], axis=1).astype(F32)


def remote_kernel(first, gains, kw, vw, q, o_in, kp_in, mine, o, kp, over, k_ref, vt_ref,
                  ones_ref):
    normed = norm_rows(first.here[:EARLY, :], gains.here[0:1, :])
    fill = far_fill(first.here)[:, :EARLY]
    keys, values_t = project_kv(normed, kw, vw, fill)
    k_ref[...] = keys
    vt_ref[...] = values_t
    ones_ref[...] = fill_rows(fill)
    kp.ref[...] = jnp.maximum(kp_in.here[...], head_peak(keys))
    kp.flush()
    used = far_fill(first.here) + far_fill(mine.here)
    over.ref[...] = jnp.broadcast_to(used[:, USUAL : USUAL + 1], (8, 128)).astype(jnp.int32)
    over.flush()
    attend(q.here, k_ref, vt_ref, ones_ref, o.ref, o_in.here)
    o.flush()


def exact_attend(level, q_ref, own, fills, chunks, counts, gains, kw, vw, att_ref, xbuf, kf, vf):
    rows = q_ref.shape[1]
    for side, sources in enumerate(([(own, rows)], list(zip(chunks, counts)))):
        at = 0
        for ref, count in sources:
            pltpu.sync_copy(ref.at[pl.ds(0, count), :], xbuf.at[pl.ds(at, count), :])
            at += count
        for start in range(0, rows, 128):
            normed = norm_rows(xbuf[start : start + 128, :], gains.here[level : level + 1, :])
            if level == 0 and side == 0:
                normed = normed * to_column(fills[0][:, start : start + 128]).astype(BF)
            keys, values_t = project_kv(normed, kw, vw)
            base = side * rows + start
            kf[base : base + 128, :] = keys
            vf[:, base : base + 128] = values_t
    total = 2 * rows
    fill8 = jnp.broadcast_to(jnp.concatenate(fills, axis=1), (8, total)).astype(BF)
    width = 128

    def body(step, carry):
        pair = step // (rows // width)
        start = pl.multiple_of(step % (rows // width) * width, width)
        lanes = pl.ds(pl.multiple_of(pair * 128, 128), 128)
        keys = kf[:, lanes]
        mask = dotf(fill8, jnp.ones((8, width), BF), TN) > 0.5
        own = lax.broadcasted_iota(jnp.int32, (total, width), 0) == (
            lax.broadcasted_iota(jnp.int32, (total, width), 1) + start
        )
        allowed = mask | own
        for head in range(2):
            queries = q_ref[2 * pair + head, pl.ds(start, width), :]
            scores = jnp.where(allowed, dotf(keys, queries, NT), -1e30)
            weights = jnp.exp(scores - jnp.max(scores, axis=0, keepdims=True))
            weights = weights / jnp.sum(weights, axis=0, keepdims=True)
            first = pl.multiple_of(pair * 128 + head * HEAD, HEAD)
            values = vf[pl.ds(first, HEAD), :]
            att_ref[pl.ds(first, HEAD), pl.ds(start, width)] = dotf(
                values, weights.astype(BF)
            ).astype(BF)
        return carry

    lax.fori_loop(0, HEADS // 2 * (rows // width), body, 0)


def finish_attention(level, far, chunk_refs, counts, operands, scratch, fill, fill_far, rest=None):
    gains, kw, vw, q, qp, kp, o, own = operands
    att_ref, k_ref, vt_ref, ones_ref, xbuf, kf, vf = scratch[:7]
    gain = gains.here[level : level + 1, :]
    begin = 0 if rest is None else EARLY
    usual = begin + k_ref.shape[0]
    normed = [norm_rows(x.here[:count, :], gain) for x, count in zip(far, counts)]
    normed = jnp.concatenate(normed, axis=0) if len(normed) > 1 else normed[0]
    keys, values_t = project_kv(normed, kw, vw, fill_far[:, begin:usual])
    k_ref[...] = keys
    vt_ref[...] = values_t
    ones_ref[...] = fill_rows(fill_far[:, begin:usual])
    attend(q.here, k_ref, vt_ref, ones_ref, o.here, o.here)
    peak = jnp.maximum(kp.here[...], head_peak(keys)) * qp.here[...]
    own.here
    if rest is not None:
        rest_k, rest_vt, rest_ones, rest_peak = scratch[7:]
        rest_peak[...] = jnp.zeros_like(rest_peak)
        rest.here

        @pl.when(jnp.max(fill_far[:, usual:]) > 0.0)
        def _():
            keys, values_t = project_kv(
                norm_rows(rest.here[...], gain), kw, vw, fill_far[:, usual:])
            rest_k[...] = keys
            rest_vt[...] = values_t
            rest_ones[...] = fill_rows(fill_far[:, usual:])
            rest_peak[...] = head_peak(keys)
            attend(q.here, rest_k, rest_vt, rest_ones, o.here, o.here)

        peak = jnp.maximum(peak, rest_peak[...] * qp.here[...])
    for head in range(HEADS):
        scale = 1.0 / o.here[head, HEAD : HEAD + 1, :]
        att_ref[head * HEAD : (head + 1) * HEAD, :] = (o.here[head, :HEAD, :] * scale).astype(BF)
    inside = jnp.max(peak) <= LIMIT2

    @pl.when(jnp.logical_not(inside))
    def _():
        exact_attend(level, q.here, own.here, [fill, fill_far], chunk_refs,
                     counts if rest is None else SENT, gains, kw, vw, att_ref, xbuf, kf, vf)

    return att_ref[...]


def finish0_kernel(*refs):
    chunks = refs[: len(SENT)]
    (packed, second, third, fill_ref, gains, kw, vw, q, o, qp, kp, ow, points, tree, rest,
     y_out, x1_out) = refs[len(SENT) : len(SENT) + 17]
    scratch = refs[len(SENT) + 17 :]
    fill = fill_ref.here[...].astype(F32)
    attended_t = finish_attention(
        0, [second, third], chunks, SENT[1:3], (gains, kw, vw, q, qp, kp, o, points), scratch,
        fill, far_fill(packed.here), rest)
    x0 = points.here[...].astype(F32) * to_column(fill)
    y = (x0 + dotf(attended_t, ow.here[...], TN)).astype(BF)
    y_out.ref[...] = y
    y_out.flush()
    f8 = jnp.broadcast_to(fill, (8, 1024)).astype(BF)
    place = tree.here[:1, :]
    fills = []
    for half in range(2):
        rows = (lax.broadcasted_iota(jnp.int32, (256, 1024), 0) + 256 * half).astype(F32)
        pool = jnp.where(rows == place, 0.5, 0.0).astype(BF)
        x1_out.ref[half * 256 : (half + 1) * 256, :] = dotf(pool, y).astype(BF)
        fills.append(jnp.where(dotf(f8, pool, NT)[:1] > 0.25, 1.0, 0.0))
    x1_out.ref[512:, :] = jnp.broadcast_to(jnp.concatenate(fills, axis=1), (16, D)).astype(BF)
    x1_out.flush()


def finish1_kernel(far_hbm, last, gains, kw, vw, q, o_in, qp, kp, x, ow, y_out, x2_out, *scratch):
    fill = x.here[512:513, :].astype(F32)
    attended_t = finish_attention(
        1, [last], [far_hbm], (512,), (gains, kw, vw, q, qp, kp, o_in, x), scratch, fill,
        last.here[512:513, :].astype(F32))
    y = (x.here[:512, :].astype(F32) + dotf(attended_t, ow.here[...], TN)).astype(BF)
    wide = y.astype(F32)
    x2_out.ref[:256, :] = ((wide[:256] + wide[256:]) * 0.5).astype(BF)
    f_next = jnp.maximum(fill[:, :256], fill[:, 256:])
    x2_out.ref[256:, :] = jnp.broadcast_to(
        jnp.concatenate([f_next, f_next], axis=1), (16, D)).astype(BF)
    x2_out.flush()
    y_out.ref[...] = y
    y_out.flush()


def finish2_kernel(far_hbm, last, gains, kw, vw, q, o_in, qp, kp, x, ow, gm, hw, pw, y1, y0, tree,
                   field, *scratch):
    fill = x.here[256:257, :256].astype(F32)
    attended_t = finish_attention(
        2, [last], [far_hbm], (256,), (gains, kw, vw, q, qp, kp, o_in, x), scratch, fill,
        last.here[256:257, :256].astype(F32))
    y2 = (x.here[:256, :].astype(F32) + dotf(attended_t, ow.here[...], TN)).astype(BF)
    normed = norm_rows(y2, gm.here[...])
    hw.here, pw.here
    total = y2.astype(F32)
    before = None
    for start in range(0, 2048 + 512, 512):
        if start < 2048:
            now = dotf(normed, hw.here[:, start : start + 512])
        if before is not None:
            hidden = jax.nn.gelu(before, approximate=True).astype(BF)
            total = total + dotf(hidden, pw.here[start - 512 : start, :])
        before = now
    top = total.astype(BF).astype(F32)
    up = [(y1.here[half * 256 : (half + 1) * 256, :].astype(F32) + top).astype(BF)
          for half in range(2)]
    place = to_column(tree.here[:1, :])
    lanes = lax.broadcasted_iota(jnp.int32, (256, 256), 1).astype(F32)
    for side, out in enumerate(field.parts(4)):
        total = y0.here[256 * side : 256 * (side + 1), :].astype(F32)
        for half in range(2):
            picked = place[256 * side : 256 * (side + 1)] == lanes + 256.0 * half
            total = total + dotf(jnp.where(picked, 1.0, 0.0).astype(BF), up[half])
        field.ref[256 * side : 256 * (side + 1), :] = total.astype(BF)
        out.start()


class Here:
    def __init__(self, ref, copy=None):
        self.here = self.ref = ref
        self.copy = copy

    def flush(self):
        if self.copy is not None:
            self.copy.start()

    def parts(self, count):
        rows = self.ref.shape[0] // count
        source, target, sem = self.ends
        return [
            pltpu.make_async_copy(
                source.at[pl.ds(i * rows, rows), :], target.at[pl.ds(i * rows, rows), :], sem)
            for i in range(count)
        ]


class Piece:
    def __init__(self, copy, ref):
        self.copy, self.ref = copy, ref

    @property
    def here(self):
        if self.copy is not None:
            self.copy.wait()
            self.copy = None
        return self.ref


def call(kernel, outs, args, raw=(), scratch=(), flops=0, limit=64, manual=False, away=()):
    arrays = [a[0] if isinstance(a, tuple) else a for a in args]
    n, m = len(args), len(outs)
    moved = [i for i in range(n) if isinstance(args[i], tuple) or (manual and i not in raw)]
    level = [args[i][1] if isinstance(args[i], tuple) else None for i in range(n)]
    buffers = [
        pltpu.VMEM(arrays[i].shape if level[i] is None else arrays[i].shape[1:], arrays[i].dtype)
        for i in moved
    ]
    away = list(range(m)) if manual else sorted(away)
    sems = [pltpu.SemaphoreType.DMA((len(moved),))] if moved else []
    if away:
        buffers = [pltpu.VMEM(outs[i].shape, outs[i].dtype) for i in away] + buffers
        sems.append(pltpu.SemaphoreType.DMA((m,)))

    def body(*refs):
        sources, targets, rest = refs[:n], refs[n : n + m], list(refs[n + m :])
        results = [Here(t) for t in targets]
        held, rest = rest[: len(away)], rest[len(away) :]
        slots, rest = rest[: len(moved)], rest[len(moved) :]
        operands = [s if i in raw else Here(s) for i, s in enumerate(sources)]
        if moved:
            sem = rest.pop(0)
        if away:
            out_sem = rest.pop(0)
        for i, h in zip(away, held):
            results[i] = Here(h, pltpu.make_async_copy(h, targets[i], out_sem.at[i]))
            results[i].ends = (h, targets[i], out_sem.at[i])
        for slot, i in enumerate(moved):
            source = sources[i] if level[i] is None else sources[i].at[level[i]]
            copy = pltpu.make_async_copy(source, slots[slot], sem.at[slot])
            copy.start()
            operands[i] = Piece(copy, slots[slot])
        kernel(*operands, *results, *rest)
        for i in moved:
            operands[i].here
        for i in away:
            results[i].copy.wait()

    nbytes = sum(a.size * a.dtype.itemsize for a in arrays) + sum(
        a.size * a.dtype.itemsize for a in outs)
    return pl.pallas_call(
        body,
        out_shape=outs,
        in_specs=[ANY if manual or i in raw or i in moved else VMEM for i in range(n)],
        out_specs=[ANY if i in away else VMEM for i in range(m)],
        scratch_shapes=buffers + sems + list(scratch),
        compiler_params=pltpu.CompilerParams(vmem_limit_bytes=limit * 2**20),
        cost_estimate=pl.CostEstimate(flops=flops, bytes_accessed=nbytes, transcendentals=0),
    )(*arrays)


def shape(*dims, dtype=BF):
    return jax.ShapeDtypeStruct(dims, dtype)


def key_scratch(rows):
    return [pltpu.VMEM((rows, D), BF), pltpu.VMEM((D, rows), BF), pltpu.VMEM((16, rows), BF)]


def local_part(level, x, fill, gains, qw, kw, vw, rows, manual, order=()):
    return call(
        functools.partial(local_kernel, level, rows),
        [shape(HEADS, rows, 128), shape(HEADS, VROWS, rows, dtype=F32),
         shape(16, 128, dtype=F32), shape(16, 128, dtype=F32)]
        + [shape(8, rows, dtype=F32) for _ in order],
        [x, fill, gains, (qw, level), (kw, level), (vw, level), *order],
        scratch=key_scratch(rows),
        flops=8 * rows * rows * 512 * 2,
        manual=manual,
        limit={0: 64, 1: 16, 2: 12}[level],
    )


def finish_part(kernel, args, raw, outs, rows, count, manual, extra=(), away=()):
    return call(
        kernel,
        outs,
        args,
        raw=set(range(raw)),
        scratch=[
            pltpu.VMEM((D, rows), BF),
            *key_scratch(count),
            pltpu.VMEM((rows, D), BF),
            pltpu.VMEM((2 * rows, D), BF),
            pltpu.VMEM((D, 2 * rows), BF),
            *extra,
        ],
        flops=8 * rows * count * 512 * 2 + 4 * rows * D * D,
        manual=manual,
        away=away,
        limit={1024: 64, 512: 16, 256: 24}[rows],
    )


def per_device(points, tree_order, present, gain_attn, query_weight, key_weight, value_weight,
               out_weight, gain_mlp, hidden_weight, proj_weight):
    size = lax.axis_size("leaf")

    def trade(value, bit):
        return lax.ppermute(value, "leaf", [(s, s ^ (1 << bit)) for s in range(size)])

    base = size.bit_length() - 1 - 3
    fill0 = present.reshape(1, 1024)
    parts = []
    for first, last in ((0, 1), (1, len(SENT))):
        parts += call(
            functools.partial(front_kernel, first),
            [shape(count + (0 if first else 16), D) for count in SENT[first:last]],
            [points, fill0], flops=10**9, manual=True)
    chunks = [trade(part, base) for part in parts[:-1]]

    def kvs(level):
        return [(key_weight, level), (value_weight, level)]

    q, o, qp, kp, spot = local_part(0, points, fill0, gain_attn, query_weight, key_weight,
                                    value_weight, 1024, True, [tree_order.reshape(1, 1024)])
    o, kp, over = call(
        remote_kernel,
        [shape(HEADS, VROWS, 1024, dtype=F32), shape(16, 128, dtype=F32),
         shape(8, 128, dtype=jnp.int32)],
        [chunks[0], gain_attn, *kvs(0), q, o, kp, parts[0]],
        scratch=key_scratch(EARLY), flops=10**10, manual=True)
    chunks.append(lax.cond(
        over[0, 0] > 0, lambda left: trade(left, base), lambda left: left, parts[-1]))
    y0, x1 = finish_part(
        finish0_kernel,
        [*chunks, *chunks[:3], fill0, gain_attn, *kvs(0), q, o, qp, kp, (out_weight, 0), points,
         spot, chunks[3]],
        len(SENT), [shape(1024, D), shape(528, D)], 1024, USUAL - EARLY, True,
        extra=[*key_scratch(SENT[-1]), pltpu.VMEM((16, 128), F32)])
    far1 = trade(x1, base + 1)
    q, o, qp, kp = local_part(1, x1, fill0, gain_attn, query_weight, key_weight, value_weight,
                              512, False)
    y1, x2 = finish_part(
        finish1_kernel,
        [far1, far1, gain_attn, *kvs(1), q, o, qp, kp, x1, (out_weight, 1)],
        1, [shape(512, D), shape(272, D)], 512, 512, False, away={0, 1})
    far2 = trade(x2, base + 2)
    q, o, qp, kp = local_part(2, x2, fill0, gain_attn, query_weight, key_weight, value_weight,
                              256, True)
    (field,) = finish_part(
        finish2_kernel,
        [far2, far2, gain_attn, *kvs(2), q, o, qp, kp, x2, (out_weight, 2),
         gain_mlp.reshape(1, D), (hidden_weight, None), (proj_weight, None), y1, y0, spot],
        1, [shape(1024, D)], 256, 256, True)
    return field


def solution(mesh):
    placed = (
        P(("cloud", "leaf"), None),
        P(("cloud", "leaf")),
        P(("cloud", "leaf")),
        P(), P(), P(), P(), P(), P(), P(), P(),
    )
    return jax.shard_map(
        per_device,
        mesh=mesh,
        in_specs=placed,
        out_specs=P(("cloud", "leaf"), None),
        check_vma=False,
    )
```
